1024 devices in a mesh: dp: 32 (over z_hi, y, core), mp: 32 (over z_lo, x).
Axes of the slice: x: 4, y: 8, z: 16 (z_hi: 2, z_lo: 8; z = z_hi * 8 + z_lo), core: 2. Of those that a mesh axis runs over, the one named last changes fastest.
Arguments:
- tokens: bfloat16 [8192, 4096], P(('dp', 'mp')), may hold values from -24 to 24
- cotangent: bfloat16 [8192, 4096], P(('dp', 'mp')), may hold values from -24 to 24
- w_qkv: bfloat16 [4096, 32, 384], P(None, 'mp'), may hold values from -0.09375 to 0.09375
- w_out: bfloat16 [32, 128, 4096], P('mp'), may hold values from -0.09375 to 0.09375
Outputs:
- grad_qkv: float32 [4096, 32, 384], P('dp', 'mp')
- grad_out: float32 [32, 128, 4096], P('mp', None, 'dp')
The draws below stay inside these ranges and needn't reach their ends.
All inputs are finite; a program needn't handle non-finite values.
Results may differ from the reference program's by a relative error of at most 0.02.
Values may be sent and summed in bfloat16 or wider, within the bound.
No kernel may reach another device: no remote copies, remote signals or barrier semaphores. Data moves between devices by JAX's collectives and lax.ppermute only.
A program may use at most 32 MiB of HBM per device.

```python
import jax
import jax.numpy as jnp
from jax import lax

D = 4096
HD = 128
PATCHES = 256
IMAGES = 1
HEADS = 32
TOKENS = 8192
N_DP = 32


def raised(array, stream_key, source, target, parts, factor):
    def block_of(axis_at):
        return (jnp.arange(array.shape[axis_at]) // (array.shape[axis_at] // parts)).reshape((-1,) + (1,) * (array.ndim - 1 - axis_at))

    first = jax.random.permutation(stream_key, parts)[block_of(target)]
    second = (block_of(target) + parts // 2) % parts
    return jnp.where((block_of(source) == first) | (block_of(source) == second), factor * array, array)


def block_scale(stream_key, shape, cuts, least, top_value):
    loudness, own = 1.0, jax.random.fold_in(stream_key, 6)
    for position, parts in cuts:
        heights = jnp.exp(jax.random.uniform(jax.random.fold_in(own, position), (parts,), jnp.float32, least / len(cuts), top_value / len(cuts)))
        loudness = loudness * jnp.repeat(heights, shape[position] // parts).reshape([-1 if axis == position else 1 for axis in range(len(shape))])
    return loudness


def noise(key, shape, scale, bound, shards=(), kind=jnp.bfloat16):
    values = jax.random.normal(key, shape, jnp.float32) * scale
    if len(shards) > 0:
        values = block_scale(key, shape, shards, -0.22, 0.18) * values
    return jnp.clip(values, min=-bound, max=bound).astype(kind)


def heavy_noise(rng, extent, scale, bound, split, heavy, kind=jnp.bfloat16):
    drawn = scale * jax.random.normal(rng, extent, jnp.float32)
    if split:
        drawn = drawn * block_scale(rng, extent, split, -0.22, 0.18)
    return jnp.clip(raised(drawn, jax.random.fold_in(rng, 3), *heavy), -bound, bound).astype(kind)


def setup_inputs(seed: int = 0) -> dict:
    key_list = jax.random.split(jax.random.key(seed), 5)
    return {
        "tokens": heavy_noise(key_list[0], (TOKENS, D), 1.0, 24.0, ((0, 1024),), (0, 1, 1024, 6.0)),
        "cotangent": heavy_noise(key_list[1], (TOKENS, D), 1.0, 24.0, ((0, 1024),), (0, 1, 1024, 6.0)),
        "w_qkv": noise(key_list[2], (D, HEADS, 3 * HD), D ** -0.5, 0.09375, ((1, 32),)),
        "w_out": noise(key_list[3], (HEADS, HD, D), (HEADS * HD) ** -0.5, 0.09375, ((0, 32),)),
    }


highest_precision = lax.Precision.HIGHEST

def normalize(values):
    centred = values - lax.optimization_barrier(jnp.mean(values, -1, keepdims=True))
    spread = lax.rsqrt(lax.optimization_barrier(jnp.mean(centred * centred, -1, keepdims=True)) + 1e-06)
    return (centred * spread, spread)

def normalize_back(grad, normed, spread):
    inner = lax.optimization_barrier(jnp.mean(grad * normed, -1, keepdims=True))
    return spread * (grad - lax.optimization_barrier(jnp.mean(grad, -1, keepdims=True)) - normed * inner)

def attend(normed, w_head, patches):
    width = w_head.shape[1] // 3
    qkv = jnp.dot(normed, w_head, preferred_element_type=jnp.float32)
    count = qkv.shape[0] // patches
    qkv = qkv.reshape(count, patches, 3 * width)
    query_rows, query_spread = normalize(qkv[..., :width])
    key, key_spread = normalize(qkv[..., width:2 * width])
    value_rows = qkv[..., 2 * width:]
    score_scale = width ** (-0.5)
    attention_scores = jnp.einsum('omx,oex->ome', query_rows, key, precision=highest_precision) * score_scale
    weights = jnp.exp(attention_scores)
    attention_probabilities = weights / lax.optimization_barrier(jnp.sum(weights, -1, keepdims=True))
    attended_values = jnp.einsum('mut,mtw->muw', attention_probabilities, value_rows, precision=highest_precision)
    attended_values = attended_values.reshape(count * patches, width).astype(jnp.bfloat16)
    return (attended_values, (query_rows, query_spread, key, key_spread, value_rows, attention_probabilities))

def attend_back(attended_gradient, saved):
    query_rows, query_spread, key, key_spread, value_rows, attention_probabilities = saved
    count, patches, width = value_rows.shape
    attended_gradient = attended_gradient.reshape(count, patches, width)
    score_scale = width ** (-0.5)
    value_gradient = jnp.einsum('wth,wtg->whg', attention_probabilities, attended_gradient, precision=highest_precision)
    probability_gradient = jnp.einsum('omx,oex->ome', attended_gradient, value_rows, precision=highest_precision)
    score_gradient = attention_probabilities * (probability_gradient - lax.optimization_barrier(jnp.sum(probability_gradient * attention_probabilities, -1, keepdims=True))) * score_scale
    query_gradient = jnp.einsum('mut,mtw->muw', score_gradient, key, precision=highest_precision)
    key_gradient = jnp.einsum('wth,wtg->whg', score_gradient, query_rows, precision=highest_precision)
    d_qkv = jnp.concatenate([normalize_back(query_gradient, query_rows, query_spread), normalize_back(key_gradient, key, key_spread), value_gradient], -1)
    return d_qkv.reshape(count * patches, 3 * width).astype(jnp.bfloat16)

def head_grads(normed, cotangent, w_head, w_back):
    attended_values, saved = attend(normed, w_head, PATCHES)
    grad_back = lax.dot_general(attended_values, cotangent, (((0,), (0,)), ((), ())), preferred_element_type=jnp.float32)
    attended_gradient = lax.dot_general(cotangent, w_back, (((1,), (1,)), ((), ())), preferred_element_type=jnp.float32)
    d_qkv = attend_back(attended_gradient, saved)
    grad_head = lax.dot_general(normed, d_qkv, (((0,), (0,)), ((), ())), preferred_element_type=jnp.float32)
    return (grad_head, grad_back)

def reference(tokens, cotangent, w_qkv, w_out):
    group_rows = IMAGES * PATCHES
    token_groups = tokens.reshape(N_DP, group_rows, D)
    cot_groups = cotangent.reshape(N_DP, group_rows, D)
    heads_first = jnp.transpose(w_qkv, (1, 0, 2))

    def one_group(totals, pair):
        rows, grads = pair
        normed = normalize(rows.astype(jnp.float32))[0].astype(jnp.bfloat16)

        def one_head(weights):
            return head_grads(normed, grads, weights[0], weights[1])
        group_qkv, group_out = lax.map(one_head, (heads_first, w_out))
        group_qkv = lax.optimization_barrier(group_qkv.astype(jnp.bfloat16)).astype(jnp.float32)
        group_out = lax.optimization_barrier(group_out.astype(jnp.bfloat16)).astype(jnp.float32)
        return ((totals[0] + group_qkv, totals[1] + group_out), None)
    start = (jnp.zeros((HEADS, D, 3 * HD), jnp.float32), jnp.zeros((HEADS, HD, D), jnp.float32))
    totals, unused = lax.scan(one_group, start, (token_groups, cot_groups))
    return (jnp.transpose(totals[0], (1, 0, 2)), totals[1])
```

```python
import functools

import jax
import jax.numpy as jnp
from jax import lax
from jax.experimental import pallas as pl
from jax.experimental.pallas import tpu as pltpu
from jax.sharding import Mesh
from jax.sharding import PartitionSpec as P

HIGHEST = lax.Precision.HIGHEST
BF16 = jnp.bfloat16
F32 = jnp.float32
EPS = 1e-6
TM = (((0,), (0,)), ((), ()))
NT = (((1,), (1,)), ((), ()))
NN = (((1,), (0,)), ((), ()))
VMEM = pl.BlockSpec(memory_space=pltpu.VMEM)
SMEM = pl.BlockSpec(memory_space=pltpu.SMEM)
PARAMS = pltpu.CompilerParams(vmem_limit_bytes=40 * 1024 * 1024)


def normalize(values):
    centred = values - jnp.mean(values, -1, keepdims=True)
    spread = lax.rsqrt(jnp.mean(centred * centred, -1, keepdims=True) + EPS)
    return centred * spread, spread


def normalize_back(grad, normed, spread):
    inner = jnp.mean(grad * normed, -1, keepdims=True)
    return spread * (grad - jnp.mean(grad, -1, keepdims=True) - normed * inner)


def exact(a, b, dims):
    return lax.dot_general(a, b, dims, precision=HIGHEST, preferred_element_type=F32)


def forward_kernel(*refs, rows):
    pieces = refs[: len(rows)]
    w_ref, normed_ref, att_ref, q_ref, k_ref, v_ref, prob_ref, sq_ref, sk_ref = refs[len(rows) :]
    step = 16
    at = 0
    for piece, count in zip(pieces, rows):

        def body(i, carry, piece=piece, at=at):
            part = pl.ds(pl.multiple_of(i * step, step), step)
            x = piece[part, :].astype(F32)
            centred = x - jnp.mean(x, -1, keepdims=True)
            spread = lax.rsqrt(jnp.mean(centred * centred, -1, keepdims=True) + EPS)
            normed_ref[pl.ds(pl.multiple_of(at + i * step, step), step), :] = (
                centred * spread
            ).astype(BF16)
            return carry

        lax.fori_loop(0, count // step, body, 0)
        at += count
    width = w_ref.shape[1] // 3
    qkv = jnp.dot(normed_ref[...], w_ref[...], preferred_element_type=F32)
    q, sq = normalize(qkv[:, :width])
    k, sk = normalize(qkv[:, width : 2 * width])
    v = qkv[:, 2 * width :]
    weights = jnp.exp(exact(q, k, NT) * width ** (-0.5))
    probs = weights / jnp.sum(weights, -1, keepdims=True)
    att_ref[...] = exact(probs, v, NN).T.astype(BF16)
    q_ref[...] = q
    k_ref[...] = k
    v_ref[...] = v
    prob_ref[...] = probs
    sq_ref[...] = jnp.broadcast_to(sq, q.shape)
    sk_ref[...] = jnp.broadcast_to(sk, k.shape)


def backward_kernel(*refs, rows):
    pieces = refs[: len(rows)]
    w_ref, q_ref, k_ref, v_ref, prob_ref, sq_ref, sk_ref, out_ref = refs[len(rows) :]
    width = w_ref.shape[0]
    cot = jnp.concatenate([piece[...] for piece in pieces], 0)
    d_att = lax.dot_general(cot, w_ref[...], NT, preferred_element_type=F32)
    q, k, v, probs = q_ref[...], k_ref[...], v_ref[...], prob_ref[...]
    d_value = exact(probs, d_att, TM)
    d_probs = exact(d_att, v, NT)
    inner = jnp.sum(d_probs * probs, -1, keepdims=True)
    d_scores = probs * (d_probs - inner) * width ** (-0.5)
    d_q = normalize_back(exact(d_scores, k, NN), q, sq_ref[...])
    d_k = normalize_back(exact(d_scores, q, TM), k, sk_ref[...])
    out_ref[:width, :] = d_q.T.astype(BF16)
    out_ref[width : 2 * width, :] = d_k.T.astype(BF16)
    out_ref[2 * width :, :] = d_value.T.astype(BF16)


def terms_kernel(*refs, count, blocks, adds):
    core_ref, normed_ref = refs[:2]
    pieces = refs[2 : 2 + count]
    d_ref, att_ref = refs[2 + count : 4 + count]
    out_ref = refs[-1]
    far, near, width = blocks
    core = core_ref[0]
    d_all, att = d_ref[...], att_ref[...]
    split = d_all.shape[0]
    for y in range(near):
        cols = [
            pl.ds(pl.multiple_of(((zh * near + y) * 2 + core) * width, width), width)
            for zh in range(far)
        ]
        rhs = jnp.concatenate([normed_ref[:, c] for c in cols], 1)
        cot = jnp.concatenate(
            [jnp.concatenate([p[:, c] for p in pieces], 0) for c in cols], 1
        )
        top = jnp.dot(d_all, rhs, preferred_element_type=F32)
        low = jnp.dot(att, cot, preferred_element_type=F32)
        for zh in range(far):
            a = top[:, zh * width : (zh + 1) * width]
            b = low[:, zh * width : (zh + 1) * width]
            if adds:
                other = refs[4 + count]
                a = a + other[y * far + zh, :split, :].astype(F32)
                b = b + other[y * far + zh, split:, :].astype(F32)
            out_ref[y * far + zh, :split, :] = a.astype(BF16)
            out_ref[y * far + zh, split:, :] = b.astype(BF16)


def swap(n, s):
    return [(i, i ^ s) for i in range(n)]


def gather_z(rows, n):
    s = n // 2
    while s:
        rows = jnp.concatenate([rows, lax.ppermute(rows, "zl", swap(n, s))], 0)
        s //= 2
    return rows


def gather_x(rows, n):
    up = [(i, (i + 1) % n) for i in range(n)]
    down = [(i, (i - 1) % n) for i in range(n)]
    half = rows.shape[0] // 2
    left = lax.ppermute(rows, "x", up)
    right = lax.ppermute(rows, "x", down)
    far_top = lax.ppermute(left[:half], "x", up)
    far_low = lax.ppermute(right[half:], "x", down)
    return [rows, left, right, far_top, far_low]


def local(sizes, tokens, cotangent, w_qkv, w_out):
    far, near, cores, n_z, n_x = sizes
    w_head = w_qkv[:, 0, :]
    w_back = w_out[0]
    model, width = w_head.shape[0], w_back.shape[0]
    t_pieces = gather_x(gather_z(tokens, n_z), n_x)
    c_pieces = gather_x(gather_z(cotangent, n_z), n_x)
    rows = tuple(p.shape[0] for p in t_pieces)
    total = sum(rows)
    small = jax.ShapeDtypeStruct((total, width), F32)
    normed, att, q, k, v, probs, sq, sk = pl.pallas_call(
        functools.partial(forward_kernel, rows=rows),
        out_shape=[
            jax.ShapeDtypeStruct((total, model), BF16),
            jax.ShapeDtypeStruct((width, total), BF16),
            small,
            small,
            small,
            jax.ShapeDtypeStruct((total, total), F32),
            small,
            small,
        ],
        in_specs=[VMEM] * (len(rows) + 1),
        out_specs=[VMEM] * 8,
        compiler_params=PARAMS,
    )(*t_pieces, w_head)
    d_qkv = pl.pallas_call(
        functools.partial(backward_kernel, rows=rows),
        out_shape=jax.ShapeDtypeStruct((3 * width, total), BF16),
        in_specs=[VMEM] * (len(rows) + 7),
        out_specs=VMEM,
        compiler_params=PARAMS,
    )(*c_pieces, w_back, q, k, v, probs, sq, sk)
    blocks = (far, near, model // (far * near * cores))

    def terms(core, *other):
        return pl.pallas_call(
            functools.partial(terms_kernel, count=len(rows), blocks=blocks, adds=len(other) > 0),
            out_shape=jax.ShapeDtypeStruct((far * near, 4 * width, blocks[2]), BF16),
            in_specs=[SMEM] + [VMEM] * (len(rows) + 3 + len(other)),
            out_specs=VMEM,
            compiler_params=PARAMS,
        )(core.reshape(1), normed, *c_pieces, d_qkv, att, *other)

    core = lax.axis_index("c").astype(jnp.int32)
    theirs = lax.ppermute(terms(1 - core), "c", swap(cores, 1))
    pair = terms(core, theirs)
    summed = lax.psum_scatter(pair, "y", scatter_dimension=0, tiled=True)
    zh = lax.axis_index("zh")
    own = lax.dynamic_index_in_dim(summed, zh, 0, keepdims=False)
    away = lax.dynamic_index_in_dim(summed, 1 - zh, 0, keepdims=False)
    both = own.astype(F32) + lax.ppermute(away, "zh", swap(far, 1)).astype(F32)
    return both[: 3 * width].T[:, None, :], both[3 * width :][None]


def solution(mesh):
    sizes = (2, mesh.shape["dp"] // 4, 2, mesh.shape["mp"] // 4, 4)
    fine = Mesh(mesh.devices.reshape(sizes), ("zh", "y", "c", "zl", "x"))
    dp, mp = ("zh", "y", "c"), ("zl", "x")
    in_specs = (P(dp + mp, None), P(dp + mp, None), P(None, mp, None), P(mp, None, None))
    out_specs = (P(dp, mp, None), P(mp, None, dp))
    return jax.shard_map(
        functools.partial(local, sizes),
        mesh=fine,
        in_specs=in_specs,
        out_specs=out_specs,
        check_vma=False,
    )
```

```python
import functools

import jax
import jax.numpy as jnp
from jax import lax
from jax.experimental import pallas as pl
from jax.experimental.pallas import tpu as pltpu
from jax.sharding import Mesh
from jax.sharding import PartitionSpec as P

HIGHEST = lax.Precision.HIGHEST
BF16 = jnp.bfloat16
F32 = jnp.float32
EPS = 1e-6
TM = (((0,), (0,)), ((), ()))
NT = (((1,), (1,)), ((), ()))
NN = (((1,), (0,)), ((), ()))
VMEM = pl.BlockSpec(memory_space=pltpu.VMEM)
SMEM = pl.BlockSpec(memory_space=pltpu.SMEM)
PARAMS = pltpu.CompilerParams(vmem_limit_bytes=16 * 1024 * 1024)


def normalize(values):
    centred = values - jnp.mean(values, -1, keepdims=True)
    spread = lax.rsqrt(jnp.mean(centred * centred, -1, keepdims=True) + EPS)
    return centred * spread, spread


def normalize_back(grad, normed, spread):
    inner = jnp.mean(grad * normed, -1, keepdims=True)
    return spread * (grad - jnp.mean(grad, -1, keepdims=True) - normed * inner)


def exact(a, b, dims):
    return lax.dot_general(a, b, dims, precision=HIGHEST, preferred_element_type=F32)


def forward_kernel(*refs, rows):
    pieces = refs[: len(rows)]
    w_ref, normed_ref, att_ref, q_ref, k_ref, v_ref, prob_ref, sq_ref, sk_ref = refs[len(rows) :]
    step = 16
    at = 0
    for piece, count in zip(pieces, rows):

        def body(i, carry, piece=piece, at=at):
            part = pl.ds(pl.multiple_of(i * step, step), step)
            x = piece[part, :].astype(F32)
            centred = x - jnp.mean(x, -1, keepdims=True)
            spread = lax.rsqrt(jnp.mean(centred * centred, -1, keepdims=True) + EPS)
            normed_ref[pl.ds(pl.multiple_of(at + i * step, step), step), :] = (
                centred * spread
            ).astype(BF16)
            return carry

        lax.fori_loop(0, count // step, body, 0)
        at += count
    width = w_ref.shape[1] // 3
    qkv = jnp.dot(normed_ref[...], w_ref[...], preferred_element_type=F32)
    q, sq = normalize(qkv[:, :width])
    k, sk = normalize(qkv[:, width : 2 * width])
    v = qkv[:, 2 * width :]
    weights = jnp.exp(exact(q, k, NT) * width ** (-0.5))
    probs = weights / jnp.sum(weights, -1, keepdims=True)
    att_ref[...] = exact(probs, v, NN).T.astype(BF16)
    q_ref[...] = q
    k_ref[...] = k
    v_ref[...] = v
    prob_ref[...] = probs
    sq_ref[...] = jnp.broadcast_to(sq, q.shape)
    sk_ref[...] = jnp.broadcast_to(sk, k.shape)


def backward_kernel(*refs, rows):
    pieces = refs[: len(rows)]
    w_ref, q_ref, k_ref, v_ref, prob_ref, sq_ref, sk_ref, out_ref = refs[len(rows) :]
    width = w_ref.shape[0]
    cot = jnp.concatenate([piece[...] for piece in pieces], 0)
    d_att = lax.dot_general(cot, w_ref[...], NT, preferred_element_type=F32)
    q, k, v, probs = q_ref[...], k_ref[...], v_ref[...], prob_ref[...]
    d_value = exact(probs, d_att, TM)
    d_probs = exact(d_att, v, NT)
    inner = jnp.sum(d_probs * probs, -1, keepdims=True)
    d_scores = probs * (d_probs - inner) * width ** (-0.5)
    d_q = normalize_back(exact(d_scores, k, NN), q, sq_ref[...])
    d_k = normalize_back(exact(d_scores, q, TM), k, sk_ref[...])
    out_ref[:width, :] = d_q.T.astype(BF16)
    out_ref[width : 2 * width, :] = d_k.T.astype(BF16)
    out_ref[2 * width :, :] = d_value.T.astype(BF16)


def terms_kernel(*refs, count, blocks, slots):
    place_ref, normed_ref = refs[:2]
    pieces = refs[2 : 2 + count]
    d_ref, att_ref = refs[2 + count : 4 + count]
    rest = refs[4 + count :]
    far, near, width = blocks
    core, here = place_ref[0], place_ref[1]
    d_all, att = d_ref[...], att_ref[...]
    split = d_all.shape[0]
    order = distances(near)
    for slot, distance in enumerate(order):
        y = lax.rem(here + distance + near, near)
        cols = [
            pl.ds(pl.multiple_of(((zh * near + y) * 2 + core) * width, width), width)
            for zh in range(far)
        ]
        rhs = jnp.concatenate([normed_ref[:, c] for c in cols], 1)
        cot = jnp.concatenate([jnp.concatenate([p[:, c] for p in pieces], 0) for c in cols], 1)
        top = jnp.dot(d_all, rhs, preferred_element_type=F32)
        low = jnp.dot(att, cot, preferred_element_type=F32)
        for zh in range(far):
            a = top[:, zh * width : (zh + 1) * width]
            b = low[:, zh * width : (zh + 1) * width]
            at = slot * far + zh
            if slots:
                other = rest[0]
                a = a + other[at, :split, :].astype(F32)
                b = b + other[at, split:, :].astype(F32)
                out = rest[1 + zh] if slot == 0 else rest[far + slot].at[zh]
            else:
                out = rest[0].at[at]
            out[:split, :] = a.astype(BF16)
            out[split:, :] = b.astype(BF16)


def distances(n):
    order = [n // 2]
    for d in range(n // 2 - 1, 0, -1):
        order += [d, -d]
    return order + [0]


def last_kernel(zh_ref, own_ref, up_ref, down_ref, away_ref, kept_ref):
    def total(at):
        return (
            own_ref[at, :, :].astype(F32)
            + up_ref[at, :, :].astype(F32)
            + down_ref[at, :, :].astype(F32)
        )

    zh = zh_ref[0]
    away_ref[...] = total(1 - zh).astype(BF16)
    kept_ref[...] = total(zh)


def finish_kernel(kept_ref, other_ref, qkv_ref, out_ref):
    both = kept_ref[...] + other_ref[...].astype(F32)
    split = qkv_ref.shape[1]
    qkv_ref[...] = both[:split].T
    out_ref[...] = both[split:]


def swap(n, s):
    return [(i, i ^ s) for i in range(n)]


def turn(n, s):
    return [(i, (i + s) % n) for i in range(n)]


def after(value, *done):
    return lax.optimization_barrier((value, *done))[0]


def gather(tokens, cotangent, n_z, n_x):
    up, down = turn(n_x, 1), turn(n_x, -1)

    def join(rows, s, *done):
        other = lax.ppermute(after(rows, *done), "zl", swap(n_z, s))
        return lax.optimization_barrier(jnp.concatenate([rows, other], 0)), other

    t, t_done = tokens, ()
    c, c_done = cotangent, ()
    s = n_z // 2
    while s > 1:
        t, other = join(t, s)
        c, last = join(c, s, *t_done)
        t_done = (other,)
        s //= 2
    tb = lax.ppermute(t, "zl", swap(n_z, 1))
    ta_left = lax.ppermute(t, "x", up)
    ta_right = lax.ppermute(t, "x", down)
    tb_right = lax.ppermute(tb, "x", down)
    tb_left = lax.ppermute(tb, "x", up)
    ta_far = lax.ppermute(ta_left, "x", up)
    tb_far = lax.ppermute(tb_right, "x", down)
    cb = lax.ppermute(after(c, tb, ta_left, ta_right), "zl", swap(n_z, 1))
    ca_left = lax.ppermute(after(c, ta_left, tb_left), "x", up)
    cb_right = lax.ppermute(after(cb, tb_right, tb_left), "x", down)
    ca_right = lax.ppermute(after(c, tb_right, tb_left), "x", down)
    cb_left = lax.ppermute(cb, "x", up)
    ca_far = lax.ppermute(ca_left, "x", up)
    cb_far = lax.ppermute(cb_right, "x", down)
    return (
        [t, ta_left, ta_right, tb, tb_left, tb_right, ta_far, tb_far],
        [c, ca_left, ca_right, cb, cb_left, cb_right, ca_far, cb_far],
    )


def local(sizes, tokens, cotangent, w_qkv, w_out):
    far, near, cores, n_z, n_x = sizes
    w_head = w_qkv[:, 0, :]
    w_back = w_out[0]
    model, width = w_head.shape[0], w_back.shape[0]
    t_pieces, c_pieces = gather(tokens, cotangent, n_z, n_x)
    rows = tuple(p.shape[0] for p in t_pieces)
    total = sum(rows)
    small = jax.ShapeDtypeStruct((total, width), F32)
    normed, att, q, k, v, probs, sq, sk = pl.pallas_call(
        functools.partial(forward_kernel, rows=rows),
        out_shape=[
            jax.ShapeDtypeStruct((total, model), BF16),
            jax.ShapeDtypeStruct((width, total), BF16),
            small,
            small,
            small,
            jax.ShapeDtypeStruct((total, total), F32),
            small,
            small,
        ],
        in_specs=[VMEM] * (len(rows) + 1),
        out_specs=[VMEM] * 8,
        compiler_params=PARAMS,
    )(*t_pieces, w_head)
    d_qkv = pl.pallas_call(
        functools.partial(backward_kernel, rows=rows),
        out_shape=jax.ShapeDtypeStruct((3 * width, total), BF16),
        in_specs=[VMEM] * (len(rows) + 7),
        out_specs=VMEM,
        compiler_params=PARAMS,
    )(*c_pieces, w_back, q, k, v, probs, sq, sk)
    blocks = (far, near, model // (far * near * cores))
    one = jax.ShapeDtypeStruct((4 * width, blocks[2]), BF16)
    two = jax.ShapeDtypeStruct((far, 4 * width, blocks[2]), BF16)
    here = lax.axis_index("y").astype(jnp.int32)
    core = lax.axis_index("c").astype(jnp.int32)

    def terms(core, shapes, *other):
        return pl.pallas_call(
            functools.partial(
                terms_kernel, count=len(rows), blocks=blocks, slots=len(other) > 0
            ),
            out_shape=shapes,
            in_specs=[SMEM] + [VMEM] * (len(rows) + 3 + len(other)),
            out_specs=[VMEM] * len(shapes),
            compiler_params=PARAMS,
        )(jnp.stack([core, here]), normed, *c_pieces, d_qkv, att, *other)

    (mine,) = terms(1 - core, [jax.ShapeDtypeStruct((far * near, 4 * width, blocks[2]), BF16)])
    theirs = lax.ppermute(mine, "c", swap(cores, 1))
    first_up, first_down, *parts = terms(core, [one, one] + [two] * (near - 1), theirs)
    ups, downs, own = parts[0:-1:2], parts[1:-1:2], parts[-1]
    up, down = turn(near, 1), turn(near, -1)

    def add(a, b):
        return (a.astype(F32) + b.astype(F32)).astype(BF16)

    goes_up = lax.ppermute(first_up, "y", up)
    goes_down = lax.ppermute(first_down, "y", down)
    for step, (a, b) in enumerate(zip(ups, downs)):
        if step == 0:
            a = jnp.stack([add(a[0], goes_up), a[1]])
            b = jnp.stack([b[0], add(b[1], goes_down)])
        else:
            a, b = add(a, goes_up), add(b, goes_down)
        goes_up = lax.ppermute(a, "y", up)
        goes_down = lax.ppermute(b, "y", down)
    away, kept = pl.pallas_call(
        last_kernel,
        out_shape=[one, jax.ShapeDtypeStruct(one.shape, F32)],
        in_specs=[SMEM] + [VMEM] * 3,
        out_specs=[VMEM] * 2,
        compiler_params=PARAMS,
    )(lax.axis_index("zh").astype(jnp.int32).reshape(1), own, goes_up, goes_down)
    other = lax.ppermute(away, "zh", swap(far, 1))
    grad_qkv, grad_out = pl.pallas_call(
        finish_kernel,
        out_shape=[
            jax.ShapeDtypeStruct((blocks[2], 3 * width), F32),
            jax.ShapeDtypeStruct((width, blocks[2]), F32),
        ],
        in_specs=[VMEM] * 2,
        out_specs=[VMEM] * 2,
        compiler_params=PARAMS,
    )(kept, other)
    return grad_qkv[:, None, :], grad_out[None]


def solution(mesh):
    sizes = (2, mesh.shape["dp"] // 4, 2, mesh.shape["mp"] // 4, 4)
    fine = Mesh(mesh.devices.reshape(sizes), ("zh", "y", "c", "zl", "x"))
    dp, mp = ("zh", "y", "c"), ("zl", "x")
    in_specs = (P(dp + mp, None), P(dp + mp, None), P(None, mp, None), P(mp, None, None))
    out_specs = (P(dp, mp, None), P(mp, None, dp))
    return jax.shard_map(
        functools.partial(local, sizes),
        mesh=fine,
        in_specs=in_specs,
        out_specs=out_specs,
        check_vma=False,
    )
```

```python
import functools

import jax
import jax.numpy as jnp
from jax import lax
from jax.experimental import pallas as pl
from jax.experimental.pallas import tpu as pltpu
from jax.sharding import Mesh
from jax.sharding import PartitionSpec as P

HIGHEST = lax.Precision.HIGHEST
BF16 = jnp.bfloat16
F32 = jnp.float32
EPS = 1e-6
TM = (((0,), (0,)), ((), ()))
NT = (((1,), (1,)), ((), ()))
NN = (((1,), (0,)), ((), ()))
VMEM = pl.BlockSpec(memory_space=pltpu.VMEM)
SMEM = pl.BlockSpec(memory_space=pltpu.SMEM)
ORDER = (4, 3, 1, -3, -1, 2, -2, 0)
PARAMS = pltpu.CompilerParams(vmem_limit_bytes=16 * 1024 * 1024)


def normalize(values):
    centred = values - jnp.mean(values, -1, keepdims=True)
    spread = lax.rsqrt(jnp.mean(centred * centred, -1, keepdims=True) + EPS)
    return centred * spread, spread


def normalize_back(grad, normed, spread):
    inner = jnp.mean(grad * normed, -1, keepdims=True)
    return spread * (grad - jnp.mean(grad, -1, keepdims=True) - normed * inner)


def exact(a, b, dims):
    return lax.dot_general(a, b, dims, precision=HIGHEST, preferred_element_type=F32)


def forward_kernel(*refs, rows):
    pieces = refs[: len(rows)]
    w_ref, normed_ref, att_ref, q_ref, k_ref, v_ref, prob_ref, sq_ref, sk_ref = refs[len(rows) :]
    step = 16
    at = 0
    for piece, count in zip(pieces, rows):

        def body(i, carry, piece=piece, at=at):
            part = pl.ds(pl.multiple_of(i * step, step), step)
            x = piece[part, :].astype(F32)
            centred = x - jnp.mean(x, -1, keepdims=True)
            spread = lax.rsqrt(jnp.mean(centred * centred, -1, keepdims=True) + EPS)
            normed_ref[pl.ds(pl.multiple_of(at + i * step, step), step), :] = (
                centred * spread
            ).astype(BF16)
            return carry

        lax.fori_loop(0, count // step, body, 0)
        at += count
    width = w_ref.shape[1] // 3
    qkv = jnp.dot(normed_ref[...], w_ref[...], preferred_element_type=F32)
    q, sq = normalize(qkv[:, :width])
    k, sk = normalize(qkv[:, width : 2 * width])
    v = qkv[:, 2 * width :]
    weights = jnp.exp(exact(q, k, NT) * width ** (-0.5))
    probs = weights / jnp.sum(weights, -1, keepdims=True)
    att_ref[...] = exact(probs, v, NN).T.astype(BF16)
    q_ref[...] = q
    k_ref[...] = k
    v_ref[...] = v
    prob_ref[...] = probs
    sq_ref[...] = jnp.broadcast_to(sq, q.shape)
    sk_ref[...] = jnp.broadcast_to(sk, k.shape)


def backward_kernel(*refs, rows):
    pieces = refs[: len(rows)]
    w_ref, q_ref, k_ref, v_ref, prob_ref, sq_ref, sk_ref, out_ref = refs[len(rows) :]
    width = w_ref.shape[0]
    cot = jnp.concatenate([piece[...] for piece in pieces], 0)
    d_att = lax.dot_general(cot, w_ref[...], NT, preferred_element_type=F32)
    q, k, v, probs = q_ref[...], k_ref[...], v_ref[...], prob_ref[...]
    d_value = exact(probs, d_att, TM)
    d_probs = exact(d_att, v, NT)
    inner = jnp.sum(d_probs * probs, -1, keepdims=True)
    d_scores = probs * (d_probs - inner) * width ** (-0.5)
    d_q = normalize_back(exact(d_scores, k, NN), q, sq_ref[...])
    d_k = normalize_back(exact(d_scores, q, TM), k, sk_ref[...])
    out_ref[:width, :] = d_q.T.astype(BF16)
    out_ref[width : 2 * width, :] = d_k.T.astype(BF16)
    out_ref[2 * width :, :] = d_value.T.astype(BF16)


def terms_kernel(*refs, count, blocks, slots):
    place_ref, normed_ref = refs[:2]
    pieces = refs[2 : 2 + count]
    d_ref, att_ref = refs[2 + count : 4 + count]
    rest = refs[4 + count :]
    far, near, width = blocks
    core, here = place_ref[0], place_ref[1]
    d_all, att = d_ref[...], att_ref[...]
    split = d_all.shape[0]
    for slot, distance in enumerate(ORDER):
        y = lax.rem(here + distance + near, near)
        cols = [
            pl.ds(pl.multiple_of(((zh * near + y) * 2 + core) * width, width), width)
            for zh in range(far)
        ]
        rhs = jnp.concatenate([normed_ref[:, c] for c in cols], 1)
        cot = jnp.concatenate([jnp.concatenate([p[:, c] for p in pieces], 0) for c in cols], 1)
        top = jnp.dot(d_all, rhs, preferred_element_type=F32)
        low = jnp.dot(att, cot, preferred_element_type=F32)
        for zh in range(far):
            a = top[:, zh * width : (zh + 1) * width]
            b = low[:, zh * width : (zh + 1) * width]
            at = slot * far + zh
            if slots:
                other = rest[0]
                a = a + other[at, :split, :].astype(F32)
                b = b + other[at, split:, :].astype(F32)
                first_up, first_down, near_up, near_down, mid_up, mid_down, own = rest[1:]
                out = {
                    4: (first_up, first_down)[zh],
                    3: near_up.at[zh],
                    1: near_up.at[far + zh],
                    -3: near_down.at[zh],
                    -1: near_down.at[far + zh],
                    2: mid_up.at[zh],
                    -2: mid_down.at[zh],
                    0: own.at[zh],
                }[distance]
            else:
                out = rest[0].at[at]
            out[:split, :] = a.astype(BF16)
            out[split:, :] = b.astype(BF16)


def middle_kernel(own_ref, near_ref, first_ref, out_ref, *, half):
    for zh in range(2):
        total = own_ref[zh, :, :].astype(F32) + near_ref[zh, :, :].astype(F32)
        if zh == half:
            total = total + first_ref[...].astype(F32)
        out_ref[zh, :, :] = total.astype(BF16)


def last_kernel(zh_ref, own_ref, near_up_ref, near_down_ref, up_ref, down_ref, away_ref, kept_ref):
    def total(at):
        near = near_up_ref[2 + at, :, :].astype(F32) + near_down_ref[2 + at, :, :].astype(F32)
        far = up_ref[at, :, :].astype(F32) + down_ref[at, :, :].astype(F32)
        return own_ref[at, :, :].astype(F32) + near + far

    zh = zh_ref[0]
    away_ref[...] = total(1 - zh).astype(BF16)
    kept_ref[...] = total(zh)


def finish_kernel(kept_ref, other_ref, qkv_ref, out_ref):
    both = kept_ref[...] + other_ref[...].astype(F32)
    split = qkv_ref.shape[1]
    qkv_ref[...] = both[:split].T
    out_ref[...] = both[split:]


def swap(n, s):
    return [(i, i ^ s) for i in range(n)]


def turn(n, s):
    return [(i, (i + s) % n) for i in range(n)]


def after(value, *done):
    return lax.optimization_barrier((value, *done))[0]


def gather(tokens, cotangent, n_z, n_x):
    up, down = turn(n_x, 1), turn(n_x, -1)

    def join(*rows):
        return lax.optimization_barrier(jnp.concatenate(rows, 0))

    def within(rows):
        return [lax.ppermute(rows, "zl", swap(n_z, s)) for s in (2, 3, 1)]

    t = join(tokens, lax.ppermute(tokens, "zl", swap(n_z, 4)))
    c = join(cotangent, lax.ppermute(cotangent, "zl", swap(n_z, 4)))
    t_near = within(t)
    c_near = within(c)
    t = join(t, *t_near)
    c = join(c, *c_near)
    t_left = lax.ppermute(t, "x", up)
    t_right = lax.ppermute(t, "x", down)
    t_far = lax.ppermute(t_left, "x", up)
    c_right = lax.ppermute(after(c, t_left, t_right), "x", down)
    c_left = lax.ppermute(after(c, t_left, t_right), "x", up)
    c_far = lax.ppermute(c_right, "x", down)
    return [t, t_left, t_right, t_far], [c, c_left, c_right, c_far]


def local(sizes, tokens, cotangent, w_qkv, w_out):
    far, near, cores, n_z, n_x = sizes
    w_head = w_qkv[:, 0, :]
    w_back = w_out[0]
    model, width = w_head.shape[0], w_back.shape[0]
    t_pieces, c_pieces = gather(tokens, cotangent, n_z, n_x)
    rows = tuple(p.shape[0] for p in t_pieces)
    total = sum(rows)
    small = jax.ShapeDtypeStruct((total, width), F32)
    normed, att, q, k, v, probs, sq, sk = pl.pallas_call(
        functools.partial(forward_kernel, rows=rows),
        out_shape=[
            jax.ShapeDtypeStruct((total, model), BF16),
            jax.ShapeDtypeStruct((width, total), BF16),
            small,
            small,
            small,
            jax.ShapeDtypeStruct((total, total), F32),
            small,
            small,
        ],
        in_specs=[VMEM] * (len(rows) + 1),
        out_specs=[VMEM] * 8,
        compiler_params=PARAMS,
    )(*t_pieces, w_head)
    d_qkv = pl.pallas_call(
        functools.partial(backward_kernel, rows=rows),
        out_shape=jax.ShapeDtypeStruct((3 * width, total), BF16),
        in_specs=[VMEM] * (len(rows) + 7),
        out_specs=VMEM,
        compiler_params=PARAMS,
    )(*c_pieces, w_back, q, k, v, probs, sq, sk)
    blocks = (far, near, model // (far * near * cores))
    one = jax.ShapeDtypeStruct((4 * width, blocks[2]), BF16)
    two = jax.ShapeDtypeStruct((far, 4 * width, blocks[2]), BF16)
    four = jax.ShapeDtypeStruct((2 * far, 4 * width, blocks[2]), BF16)
    here = lax.axis_index("y").astype(jnp.int32)
    core = lax.axis_index("c").astype(jnp.int32)

    def terms(core, shapes, *other):
        return pl.pallas_call(
            functools.partial(
                terms_kernel, count=len(rows), blocks=blocks, slots=len(other) > 0
            ),
            out_shape=shapes,
            in_specs=[SMEM] + [VMEM] * (len(rows) + 3 + len(other)),
            out_specs=[VMEM] * len(shapes),
            compiler_params=PARAMS,
        )(jnp.stack([core, here]), normed, *c_pieces, d_qkv, att, *other)

    (mine,) = terms(1 - core, [jax.ShapeDtypeStruct((far * near, 4 * width, blocks[2]), BF16)])
    theirs = lax.ppermute(mine, "c", swap(cores, 1))
    first_up, first_down, near_up, near_down, mid_up, mid_down, own = terms(
        core, [one, one, four, four, two, two, two], theirs
    )
    first_up = lax.ppermute(first_up, "y", turn(near, 2))
    near_up = lax.ppermute(near_up, "y", turn(near, 1))
    first_down = lax.ppermute(first_down, "y", turn(near, -2))
    near_down = lax.ppermute(near_down, "y", turn(near, -1))

    def middle(half, *args):
        return pl.pallas_call(
            functools.partial(middle_kernel, half=half),
            out_shape=two,
            in_specs=[VMEM] * 3,
            out_specs=VMEM,
            compiler_params=PARAMS,
        )(*args)

    goes_up = lax.ppermute(middle(0, mid_up, near_up, first_up), "y", turn(near, 2))
    goes_down = lax.ppermute(middle(1, mid_down, near_down, first_down), "y", turn(near, -2))
    away, kept = pl.pallas_call(
        last_kernel,
        out_shape=[one, jax.ShapeDtypeStruct(one.shape, F32)],
        in_specs=[SMEM] + [VMEM] * 5,
        out_specs=[VMEM] * 2,
        compiler_params=PARAMS,
    )(
        lax.axis_index("zh").astype(jnp.int32).reshape(1),
        own,
        near_up,
        near_down,
        goes_up,
        goes_down,
    )
    other = lax.ppermute(away, "zh", swap(far, 1))
    grad_qkv, grad_out = pl.pallas_call(
        finish_kernel,
        out_shape=[
            jax.ShapeDtypeStruct((blocks[2], 3 * width), F32),
            jax.ShapeDtypeStruct((width, blocks[2]), F32),
        ],
        in_specs=[VMEM] * 2,
        out_specs=[VMEM] * 2,
        compiler_params=PARAMS,
    )(kept, other)
    return grad_qkv[:, None, :], grad_out[None]


def solution(mesh):
    sizes = (2, mesh.shape["dp"] // 4, 2, mesh.shape["mp"] // 4, 4)
    fine = Mesh(mesh.devices.reshape(sizes), ("zh", "y", "c", "zl", "x"))
    dp, mp = ("zh", "y", "c"), ("zl", "x")
    in_specs = (P(dp + mp, None), P(dp + mp, None), P(None, mp, None), P(mp, None, None))
    out_specs = (P(dp, mp, None), P(mp, None, dp))
    return jax.shard_map(
        functools.partial(local, sizes),
        mesh=fine,
        in_specs=in_specs,
        out_specs=out_specs,
        check_vma=False,
    )
```

```python
import functools

import jax
import jax.numpy as jnp
from jax import lax
from jax.experimental import pallas as pl
from jax.experimental.pallas import tpu as pltpu
from jax.sharding import Mesh
from jax.sharding import PartitionSpec as P

HIGHEST = lax.Precision.HIGHEST
BF16 = jnp.bfloat16
F32 = jnp.float32
EPS = 1e-6
TM = (((0,), (0,)), ((), ()))
NT = (((1,), (1,)), ((), ()))
NN = (((1,), (0,)), ((), ()))
VMEM = pl.BlockSpec(memory_space=pltpu.VMEM)
SMEM = pl.BlockSpec(memory_space=pltpu.SMEM)
FIRST, SECOND = (4, 3, -3), (2, -2, 1, -1, 0)
PARAMS = pltpu.CompilerParams(vmem_limit_bytes=16 * 1024 * 1024)


def normalize(values):
    centred = values - jnp.mean(values, -1, keepdims=True)
    spread = lax.rsqrt(jnp.mean(centred * centred, -1, keepdims=True) + EPS)
    return centred * spread, spread


def normalize_back(grad, normed, spread):
    inner = jnp.mean(grad * normed, -1, keepdims=True)
    return spread * (grad - jnp.mean(grad, -1, keepdims=True) - normed * inner)


def exact(a, b, dims):
    return lax.dot_general(a, b, dims, precision=HIGHEST, preferred_element_type=F32)


def normalize_rows(piece, normed_ref, at, count):
    step = 16

    def body(i, carry):
        x = piece[pl.ds(pl.multiple_of(i * step, step), step), :].astype(F32)
        centred = x - jnp.mean(x, -1, keepdims=True)
        spread = lax.rsqrt(jnp.mean(centred * centred, -1, keepdims=True) + EPS)
        rows = pl.ds(pl.multiple_of(at + i * step, step), step)
        normed_ref[rows, :] = (centred * spread).astype(BF16)
        return carry

    lax.fori_loop(0, count // step, body, 0)


def own_kernel(rows_ref, normed_ref):
    normalize_rows(rows_ref, normed_ref, 0, rows_ref.shape[0])


def forward_kernel(*refs, rows):
    own_ref, *pieces = refs[: len(rows)]
    w_ref, normed_ref, att_ref, q_ref, k_ref, v_ref, prob_ref, sq_ref, sk_ref = refs[len(rows) :]
    at = rows[0]
    normed_ref[:at, :] = own_ref[...]
    for piece, count in zip(pieces, rows[1:]):
        normalize_rows(piece, normed_ref, at, count)
        at += count
    width = w_ref.shape[1] // 3
    qkv = jnp.dot(normed_ref[...], w_ref[...], preferred_element_type=F32)
    q, sq = normalize(qkv[:, :width])
    k, sk = normalize(qkv[:, width : 2 * width])
    v = qkv[:, 2 * width :]
    weights = jnp.exp(exact(q, k, NT) * width ** (-0.5))
    probs = weights / jnp.sum(weights, -1, keepdims=True)
    att_ref[...] = exact(probs, v, NN).T.astype(BF16)
    q_ref[...] = q
    k_ref[...] = k
    v_ref[...] = v
    prob_ref[...] = probs
    sq_ref[...] = jnp.broadcast_to(sq, q.shape)
    sk_ref[...] = jnp.broadcast_to(sk, k.shape)


def backward_kernel(*refs, rows):
    pieces = refs[: len(rows)]
    w_ref, q_ref, k_ref, v_ref, prob_ref, sq_ref, sk_ref, out_ref = refs[len(rows) :]
    width = w_ref.shape[0]
    cot = jnp.concatenate([piece[...] for piece in pieces], 0)
    d_att = lax.dot_general(cot, w_ref[...], NT, preferred_element_type=F32)
    q, k, v, probs = q_ref[...], k_ref[...], v_ref[...], prob_ref[...]
    d_value = exact(probs, d_att, TM)
    d_probs = exact(d_att, v, NT)
    inner = jnp.sum(d_probs * probs, -1, keepdims=True)
    d_scores = probs * (d_probs - inner) * width ** (-0.5)
    d_q = normalize_back(exact(d_scores, k, NN), q, sq_ref[...])
    d_k = normalize_back(exact(d_scores, q, TM), k, sk_ref[...])
    out_ref[:width, :] = d_q.T.astype(BF16)
    out_ref[width : 2 * width, :] = d_k.T.astype(BF16)
    out_ref[2 * width :, :] = d_value.T.astype(BF16)


def terms_kernel(*refs, count, blocks, order, adds):
    place_ref, normed_ref = refs[:2]
    pieces = refs[2 : 2 + count]
    d_ref, att_ref = refs[2 + count : 4 + count]
    rest = refs[4 + count :]
    far, near, width = blocks
    core, here = place_ref[0], place_ref[1]
    d_all, att = d_ref[...], att_ref[...]
    split = d_all.shape[0]
    if adds:
        other, outs = rest[0], []
        rest = list(rest[1:])
        for distance in order:
            if distance == near // 2:
                outs.append([rest.pop(0), rest.pop(0)])
            else:
                block = rest.pop(0)
                outs.append([block.at[zh] for zh in range(far)])
    else:
        outs = [[rest[0].at[slot * far + zh] for zh in range(far)] for slot in range(len(order))]
    for slot, distance in enumerate(order):
        y = lax.rem(here + distance + near, near)
        cols = [
            pl.ds(pl.multiple_of(((zh * near + y) * 2 + core) * width, width), width)
            for zh in range(far)
        ]
        rhs = jnp.concatenate([normed_ref[:, c] for c in cols], 1)
        cot = jnp.concatenate([jnp.concatenate([p[:, c] for p in pieces], 0) for c in cols], 1)
        top = jnp.dot(d_all, rhs, preferred_element_type=F32)
        low = jnp.dot(att, cot, preferred_element_type=F32)
        for zh in range(far):
            a = top[:, zh * width : (zh + 1) * width]
            b = low[:, zh * width : (zh + 1) * width]
            if adds:
                a = a + other[slot * far + zh, :split, :].astype(F32)
                b = b + other[slot * far + zh, split:, :].astype(F32)
            outs[slot][zh][:split, :] = a.astype(BF16)
            outs[slot][zh][split:, :] = b.astype(BF16)


def hop_kernel(own_ref, came_ref, out_ref, *, half):
    for zh in range(2):
        total = own_ref[zh, :, :].astype(F32)
        if half is None:
            total = total + came_ref[zh, :, :].astype(F32)
        elif zh == half:
            total = total + came_ref[...].astype(F32)
        out_ref[zh, :, :] = total.astype(BF16)


def last_kernel(zh_ref, own_ref, up_ref, down_ref, away_ref, kept_ref):
    def total(at):
        came = up_ref[at, :, :].astype(F32) + down_ref[at, :, :].astype(F32)
        return own_ref[at, :, :].astype(F32) + came

    zh = zh_ref[0]
    away_ref[...] = total(1 - zh).astype(BF16)
    kept_ref[...] = total(zh)


def finish_kernel(kept_ref, other_ref, qkv_ref, out_ref):
    both = kept_ref[...] + other_ref[...].astype(F32)
    split = qkv_ref.shape[1]
    qkv_ref[...] = both[:split].T
    out_ref[...] = both[split:]


def swap(n, s):
    return [(i, i ^ s) for i in range(n)]


def turn(n, s):
    return [(i, (i + s) % n) for i in range(n)]


def after(value, *done):
    return lax.optimization_barrier((value, *done))[0]


def gather(tokens, cotangent, n_z, n_x):
    up, down = turn(n_x, 1), turn(n_x, -1)

    def join(*rows):
        return lax.optimization_barrier(jnp.concatenate(rows, 0))

    def within(rows):
        return [lax.ppermute(rows, "zl", swap(n_z, s)) for s in (2, 3, 1)]

    t_other = lax.ppermute(tokens, "zl", swap(n_z, 4))
    t = join(tokens, t_other)
    t_near = within(t)
    c = join(cotangent, lax.ppermute(after(cotangent, t), "zl", swap(n_z, 4)))
    t = join(t, *t_near)
    t_left = lax.ppermute(t, "x", up)
    t_right = lax.ppermute(t, "x", down)
    normed = pl.pallas_call(
        own_kernel,
        out_shape=jax.ShapeDtypeStruct(t.shape, BF16),
        in_specs=[VMEM],
        out_specs=VMEM,
        compiler_params=PARAMS,
    )(t)
    c_near = within(after(c, normed))
    c = join(after(c, t_left, t_right), *c_near)
    t_far = lax.ppermute(t_left, "x", up)
    c_right = lax.ppermute(after(c, t_left, t_right), "x", down)
    c_left = lax.ppermute(after(c, t_left, t_right), "x", up)
    c_far = lax.ppermute(c_right, "x", down)
    return [normed, t_left, t_right, t_far], [c, c_left, c_right, c_far]


def local(sizes, tokens, cotangent, w_qkv, w_out):
    far, near, cores, n_z, n_x = sizes
    w_head = w_qkv[:, 0, :]
    w_back = w_out[0]
    model, width = w_head.shape[0], w_back.shape[0]
    t_pieces, c_pieces = gather(tokens, cotangent, n_z, n_x)
    rows = tuple(p.shape[0] for p in t_pieces)
    total = sum(rows)
    small = jax.ShapeDtypeStruct((total, width), F32)
    normed, att, q, k, v, probs, sq, sk = pl.pallas_call(
        functools.partial(forward_kernel, rows=rows),
        out_shape=[
            jax.ShapeDtypeStruct((total, model), BF16),
            jax.ShapeDtypeStruct((width, total), BF16),
            small,
            small,
            small,
            jax.ShapeDtypeStruct((total, total), F32),
            small,
            small,
        ],
        in_specs=[VMEM] * (len(rows) + 1),
        out_specs=[VMEM] * 8,
        compiler_params=PARAMS,
    )(*t_pieces, w_head)
    d_qkv = pl.pallas_call(
        functools.partial(backward_kernel, rows=rows),
        out_shape=jax.ShapeDtypeStruct((3 * width, total), BF16),
        in_specs=[VMEM] * (len(rows) + 7),
        out_specs=VMEM,
        compiler_params=PARAMS,
    )(*c_pieces, w_back, q, k, v, probs, sq, sk)
    blocks = (far, near, model // (far * near * cores))
    one = jax.ShapeDtypeStruct((4 * width, blocks[2]), BF16)
    two = jax.ShapeDtypeStruct((far, 4 * width, blocks[2]), BF16)
    here = lax.axis_index("y").astype(jnp.int32)
    core = lax.axis_index("c").astype(jnp.int32)

    def terms(core, order, *other):
        adds = len(other) > 0
        if adds:
            shapes = []
            for distance in order:
                shapes += [one, one] if distance == near // 2 else [two]
        else:
            shapes = [jax.ShapeDtypeStruct((far * len(order), 4 * width, blocks[2]), BF16)]
        return pl.pallas_call(
            functools.partial(
                terms_kernel, count=len(rows), blocks=blocks, order=order, adds=adds
            ),
            out_shape=shapes,
            in_specs=[SMEM] + [VMEM] * (len(rows) + 3 + len(other)),
            out_specs=[VMEM] * len(shapes),
            compiler_params=PARAMS,
        )(jnp.stack([core, here]), normed, *c_pieces, d_qkv, att, *other)

    (sent_first,) = terms(1 - core, FIRST)
    theirs_first = lax.ppermute(sent_first, "c", swap(cores, 1))
    (sent,) = terms(1 - core, SECOND)
    theirs = lax.ppermute(after(sent, theirs_first), "c", swap(cores, 1))
    up, down = turn(near, 1), turn(near, -1)
    goes_up, goes_down, up_3, down_3 = terms(core, FIRST, theirs_first)
    goes_up = lax.ppermute(goes_up, "y", up)
    goes_down = lax.ppermute(goes_down, "y", down)
    up_2, down_2, up_1, down_1, own = terms(core, SECOND, theirs)

    def hop(half, *args):
        return pl.pallas_call(
            functools.partial(hop_kernel, half=half),
            out_shape=two,
            in_specs=[VMEM] * 2,
            out_specs=VMEM,
            compiler_params=PARAMS,
        )(*args)

    for a, b, halves in ((up_3, down_3, (0, 1)), (up_2, down_2, (None, None)), (up_1, down_1, (None, None))):
        goes_up = lax.ppermute(hop(halves[0], a, goes_up), "y", up)
        goes_down = lax.ppermute(hop(halves[1], b, goes_down), "y", down)
    away, kept = pl.pallas_call(
        last_kernel,
        out_shape=[one, jax.ShapeDtypeStruct(one.shape, F32)],
        in_specs=[SMEM] + [VMEM] * 3,
        out_specs=[VMEM] * 2,
        compiler_params=PARAMS,
    )(lax.axis_index("zh").astype(jnp.int32).reshape(1), own, goes_up, goes_down)
    other = lax.ppermute(away, "zh", swap(far, 1))
    grad_qkv, grad_out = pl.pallas_call(
        finish_kernel,
        out_shape=[
            jax.ShapeDtypeStruct((blocks[2], 3 * width), F32),
            jax.ShapeDtypeStruct((width, blocks[2]), F32),
        ],
        in_specs=[VMEM] * 2,
        out_specs=[VMEM] * 2,
        compiler_params=PARAMS,
    )(kept, other)
    return grad_qkv[:, None, :], grad_out[None]


def solution(mesh):
    sizes = (2, mesh.shape["dp"] // 4, 2, mesh.shape["mp"] // 4, 4)
    fine = Mesh(mesh.devices.reshape(sizes), ("zh", "y", "c", "zl", "x"))
    dp, mp = ("zh", "y", "c"), ("zl", "x")
    in_specs = (P(dp + mp, None), P(dp + mp, None), P(None, mp, None), P(mp, None, None))
    out_specs = (P(dp, mp, None), P(mp, None, dp))
    return jax.shard_map(
        functools.partial(local, sizes),
        mesh=fine,
        in_specs=in_specs,
        out_specs=out_specs,
        check_vma=False,
    )
```

```python
import functools

import jax
import jax.numpy as jnp
from jax import lax
from jax.experimental import pallas as pl
from jax.experimental.pallas import tpu as pltpu
from jax.sharding import Mesh
from jax.sharding import PartitionSpec as P

HIGHEST = lax.Precision.HIGHEST
BF16 = jnp.bfloat16
F32 = jnp.float32
EPS = 1e-6
TM = (((0,), (0,)), ((), ()))
NT = (((1,), (1,)), ((), ()))
NN = (((1,), (0,)), ((), ()))
VMEM = pl.BlockSpec(memory_space=pltpu.VMEM)
SMEM = pl.BlockSpec(memory_space=pltpu.SMEM)
ORDER = (4, 3, -3, 2, -2, 1, -1, 0)
PARAMS = pltpu.CompilerParams(vmem_limit_bytes=16 * 1024 * 1024)


def normalize(values):
    centred = values - jnp.mean(values, -1, keepdims=True)
    spread = lax.rsqrt(jnp.mean(centred * centred, -1, keepdims=True) + EPS)
    return centred * spread, spread


def normalize_back(grad, normed, spread):
    inner = jnp.mean(grad * normed, -1, keepdims=True)
    return spread * (grad - jnp.mean(grad, -1, keepdims=True) - normed * inner)


def exact(a, b, dims):
    return lax.dot_general(a, b, dims, precision=HIGHEST, preferred_element_type=F32)


def normalize_rows(piece, normed_ref, at, count):
    step = 16

    def body(i, carry):
        x = piece[pl.ds(pl.multiple_of(i * step, step), step), :].astype(F32)
        centred = x - jnp.mean(x, -1, keepdims=True)
        spread = lax.rsqrt(jnp.mean(centred * centred, -1, keepdims=True) + EPS)
        rows = pl.ds(pl.multiple_of(at + i * step, step), step)
        normed_ref[rows, :] = (centred * spread).astype(BF16)
        return carry

    lax.fori_loop(0, count // step, body, 0)


def normalize_kernel(*refs):
    normed_ref, at = refs[-1], 0
    for piece in refs[:-1]:
        normalize_rows(piece, normed_ref, at, piece.shape[0])
        at += piece.shape[0]


def forward_kernel(*refs, count):
    pieces = refs[:count]
    w_ref, att_ref, q_ref, k_ref, v_ref, prob_ref, sq_ref, sk_ref = refs[count:]
    width = w_ref.shape[1] // 3
    qkv = jnp.concatenate(
        [jnp.dot(p[...], w_ref[...], preferred_element_type=F32) for p in pieces], 0
    )
    q, sq = normalize(qkv[:, :width])
    k, sk = normalize(qkv[:, width : 2 * width])
    v = qkv[:, 2 * width :]
    weights = jnp.exp(exact(q, k, NT) * width ** (-0.5))
    probs = weights / jnp.sum(weights, -1, keepdims=True)
    att_ref[...] = exact(probs, v, NN).T.astype(BF16)
    q_ref[...] = q
    k_ref[...] = k
    v_ref[...] = v
    prob_ref[...] = probs
    sq_ref[...] = jnp.broadcast_to(sq, q.shape)
    sk_ref[...] = jnp.broadcast_to(sk, k.shape)


def backward_kernel(*refs, count):
    pieces = refs[:count]
    w_ref, q_ref, k_ref, v_ref, prob_ref, sq_ref, sk_ref, out_ref = refs[count:]
    width = w_ref.shape[0]
    cot = jnp.concatenate([piece[...] for piece in pieces], 0)
    d_att = lax.dot_general(cot, w_ref[...], NT, preferred_element_type=F32)
    q, k, v, probs = q_ref[...], k_ref[...], v_ref[...], prob_ref[...]
    d_value = exact(probs, d_att, TM)
    d_probs = exact(d_att, v, NT)
    inner = jnp.sum(d_probs * probs, -1, keepdims=True)
    d_scores = probs * (d_probs - inner) * width ** (-0.5)
    d_q = normalize_back(exact(d_scores, k, NN), q, sq_ref[...])
    d_k = normalize_back(exact(d_scores, q, TM), k, sk_ref[...])
    out_ref[:width, :] = d_q.T.astype(BF16)
    out_ref[width : 2 * width, :] = d_k.T.astype(BF16)
    out_ref[2 * width :, :] = d_value.T.astype(BF16)


def terms_kernel(*refs, counts, blocks):
    place_ref, refs = refs[0], refs[1:]
    normed, pieces = refs[: counts[0]], refs[counts[0] : sum(counts)]
    d_ref, att_ref, out_ref = refs[sum(counts) :]
    far, near, width = blocks
    core, here, zh = place_ref[0], place_ref[1], place_ref[2]
    d_all, att = d_ref[...], att_ref[...]
    split = d_all.shape[0]
    for slot, distance in enumerate(ORDER):
        y = lax.rem(here + distance + near, near)
        cols = [
            pl.ds(pl.multiple_of(((z * near + y) * 2 + core) * width, width), width)
            for z in (1 - zh, zh)
        ]
        rhs = jnp.concatenate([jnp.concatenate([p[:, c] for p in normed], 0) for c in cols], 1)
        cot = jnp.concatenate([jnp.concatenate([p[:, c] for p in pieces], 0) for c in cols], 1)
        top = jnp.dot(d_all, rhs, preferred_element_type=F32)
        low = jnp.dot(att, cot, preferred_element_type=F32)
        for i in range(far):
            out_ref[slot * far + i, :split, :] = top[:, i * width : (i + 1) * width].astype(BF16)
            out_ref[slot * far + i, split:, :] = low[:, i * width : (i + 1) * width].astype(BF16)


def sum_kernel(*refs, ats):
    own_ref, theirs_ref, *came = refs[: len(refs) - len(ats)]
    for out_ref, at in zip(refs[len(refs) - len(ats) :], ats):
        total = own_ref[at, :, :].astype(F32) + theirs_ref[at, :, :].astype(F32)
        for ref in came:
            total = total + ref[...].astype(F32)
        out_ref[...] = total.astype(BF16)


def finish_kernel(own_ref, theirs_ref, up_ref, down_ref, other_ref, qkv_ref, out_ref, *, at):
    both = own_ref[at, :, :].astype(F32) + theirs_ref[at, :, :].astype(F32)
    for ref in (up_ref, down_ref, other_ref):
        both = both + ref[...].astype(F32)
    split = qkv_ref.shape[-1]
    qkv_ref[:, 0, :] = both[:split].T
    out_ref[0, :, :] = both[split:]


def swap(n, s):
    return [(i, i ^ s) for i in range(n)]


def turn(n, s):
    return [(i, (i + s) % n) for i in range(n)]


def after(value, *done):
    return lax.optimization_barrier((value, *done))[0]


def normalized(*pieces):
    rows = sum(p.shape[0] for p in pieces)
    return pl.pallas_call(
        normalize_kernel,
        out_shape=jax.ShapeDtypeStruct((rows, pieces[0].shape[1]), BF16),
        in_specs=[VMEM] * len(pieces),
        out_specs=VMEM,
        compiler_params=PARAMS,
    )(*pieces)


def gather(tokens, cotangent, n_z, n_x):
    up, down = turn(n_x, 1), turn(n_x, -1)

    def join(*rows):
        return lax.optimization_barrier(jnp.concatenate(rows, 0))

    def within(rows):
        return [lax.ppermute(rows, "zl", swap(n_z, s)) for s in (2, 3, 1)]

    t_other = lax.ppermute(tokens, "zl", swap(n_z, 4))
    t = join(tokens, t_other)
    t_near = within(t)
    c = join(cotangent, lax.ppermute(after(cotangent, t), "zl", swap(n_z, 4)))
    t = join(t, *t_near)
    t_left = lax.ppermute(t, "x", up)
    t_right = lax.ppermute(t, "x", down)
    normed = normalized(t)
    c_near = within(after(c, normed))
    half = t.shape[0] // 2
    t_top, t_low = lax.optimization_barrier((t_left[:half], t_right[half:]))
    c = join(after(c, t_top, t_low), *c_near)
    t_top = lax.ppermute(t_top, "x", up)
    t_low = lax.ppermute(t_low, "x", down)
    c = after(c, t_top, t_low)
    c_right = lax.ppermute(c, "x", down)
    c_left = lax.ppermute(c, "x", up)
    return [normed, normalized(t_left, t_right, t_top, t_low)], [c, c_left, c_right]


def far_halves(pieces, n_x, *done):
    rows, left, right = pieces
    half = rows.shape[0] // 2
    top = lax.ppermute(after(left, *done)[:half], "x", turn(n_x, 1))
    low = lax.ppermute(after(right, *done)[half:], "x", turn(n_x, -1))
    return [rows, left, right, top, low]


def local(sizes, tokens, cotangent, w_qkv, w_out):
    far, near, cores, n_z, n_x = sizes
    w_head = w_qkv[:, 0, :]
    w_back = w_out[0]
    model, width = w_head.shape[0], w_back.shape[0]
    normed, c_pieces = gather(tokens, cotangent, n_z, n_x)
    c_pieces = far_halves(c_pieces, n_x, normed[-1])
    total = sum(p.shape[0] for p in normed)
    small = jax.ShapeDtypeStruct((total, width), F32)
    att, *saved = pl.pallas_call(
        functools.partial(forward_kernel, count=len(normed)),
        out_shape=[
            jax.ShapeDtypeStruct((width, total), BF16),
            small,
            small,
            small,
            jax.ShapeDtypeStruct((total, total), F32),
            small,
            small,
        ],
        in_specs=[VMEM] * (len(normed) + 1),
        out_specs=[VMEM] * 7,
        compiler_params=PARAMS,
    )(*normed, w_head)
    d_qkv = pl.pallas_call(
        functools.partial(backward_kernel, count=len(c_pieces)),
        out_shape=jax.ShapeDtypeStruct((3 * width, total), BF16),
        in_specs=[VMEM] * (len(c_pieces) + 7),
        out_specs=VMEM,
        compiler_params=PARAMS,
    )(*c_pieces, w_back, *saved)
    blocks = (far, near, model // (far * near * cores))
    one = jax.ShapeDtypeStruct((4 * width, blocks[2]), BF16)
    here = lax.axis_index("y").astype(jnp.int32)
    core = lax.axis_index("c").astype(jnp.int32)
    zh = lax.axis_index("zh").astype(jnp.int32)

    def terms(core):
        return pl.pallas_call(
            functools.partial(
                terms_kernel, counts=(len(normed), len(c_pieces)), blocks=blocks
            ),
            out_shape=jax.ShapeDtypeStruct((far * near, *one.shape), BF16),
            in_specs=[SMEM] + [VMEM] * (len(normed) + len(c_pieces) + 2),
            out_specs=VMEM,
            compiler_params=PARAMS,
        )(jnp.stack([core, here, zh]), *normed, *c_pieces, d_qkv, att)

    theirs = lax.ppermute(terms(1 - core), "c", swap(cores, 1))
    mine = terms(core)

    def place(distance, kept):
        return ORDER.index(distance) * far + kept

    def added(ats, *came):
        return pl.pallas_call(
            functools.partial(sum_kernel, ats=ats),
            out_shape=[one] * len(ats),
            in_specs=[VMEM] * (2 + len(came)),
            out_specs=[VMEM] * len(ats),
            compiler_params=PARAMS,
        )(mine, theirs, *came)

    chains = [(4, 1, 0), (3, -1, 0), (4, -1, 1), (3, 1, 1)]
    first = added([place(n if n == 4 else n * way, kept) for n, way, kept in chains])
    came = {}
    for step in range(4):
        for at, (n, way, kept) in enumerate(chains):
            left = n - step
            if left < 1:
                continue
            if step == 0:
                message = first[at]
            else:
                (message,) = added([place(left * way, kept)], came[way, kept])
            came[way, kept] = lax.ppermute(message, "y", turn(near, way))
    (away,) = added([place(0, 0)], came[1, 0], came[-1, 0])
    other = lax.ppermute(away, "zh", swap(far, 1))
    return pl.pallas_call(
        functools.partial(finish_kernel, at=place(0, 1)),
        out_shape=[
            jax.ShapeDtypeStruct((blocks[2], 1, 3 * width), F32),
            jax.ShapeDtypeStruct((1, width, blocks[2]), F32),
        ],
        in_specs=[VMEM] * 5,
        out_specs=[VMEM] * 2,
        compiler_params=PARAMS,
    )(mine, theirs, came[1, 1], came[-1, 1], other)


def solution(mesh):
    sizes = (2, mesh.shape["dp"] // 4, 2, mesh.shape["mp"] // 4, 4)
    fine = Mesh(mesh.devices.reshape(sizes), ("zh", "y", "c", "zl", "x"))
    dp, mp = ("zh", "y", "c"), ("zl", "x")
    in_specs = (P(dp + mp, None), P(dp + mp, None), P(None, mp, None), P(mp, None, None))
    out_specs = (P(dp, mp, None), P(mp, None, dp))
    return jax.shard_map(
        functools.partial(local, sizes),
        mesh=fine,
        in_specs=in_specs,
        out_specs=out_specs,
        check_vma=False,
    )
```

```python
import functools

import jax
import jax.numpy as jnp
from jax import lax
from jax.experimental import pallas as pl
from jax.experimental.pallas import tpu as pltpu
from jax.sharding import Mesh
from jax.sharding import PartitionSpec as P

HIGHEST = lax.Precision.HIGHEST
BF16 = jnp.bfloat16
F32 = jnp.float32
EPS = 1e-6
TM = (((0,), (0,)), ((), ()))
NT = (((1,), (1,)), ((), ()))
NN = (((1,), (0,)), ((), ()))
VMEM = pl.BlockSpec(memory_space=pltpu.VMEM)
SMEM = pl.BlockSpec(memory_space=pltpu.SMEM)
ORDER = (4, 3, -3, 2, -2, 1, -1, 0)
PARAMS = pltpu.CompilerParams(vmem_limit_bytes=16 * 1024 * 1024)


def normalize(values):
    centred = values - jnp.mean(values, -1, keepdims=True)
    spread = lax.rsqrt(jnp.mean(centred * centred, -1, keepdims=True) + EPS)
    return centred * spread, spread


def normalize_back(grad, normed, spread):
    inner = jnp.mean(grad * normed, -1, keepdims=True)
    return spread * (grad - jnp.mean(grad, -1, keepdims=True) - normed * inner)


def exact(a, b, dims):
    return lax.dot_general(a, b, dims, precision=HIGHEST, preferred_element_type=F32)


def normalize_rows(piece, normed_ref, at, count):
    step = 16

    def body(i, carry):
        x = piece[pl.ds(pl.multiple_of(i * step, step), step), :].astype(F32)
        centred = x - jnp.mean(x, -1, keepdims=True)
        spread = lax.rsqrt(jnp.mean(centred * centred, -1, keepdims=True) + EPS)
        rows = pl.ds(pl.multiple_of(at + i * step, step), step)
        normed_ref[rows, :] = (centred * spread).astype(BF16)
        return carry

    lax.fori_loop(0, count // step, body, 0)


def normalize_kernel(*refs):
    normed_ref, at = refs[-1], 0
    for piece in refs[:-1]:
        normalize_rows(piece, normed_ref, at, piece.shape[0])
        at += piece.shape[0]


def forward_kernel(*refs, count):
    pieces = refs[:count]
    w_ref, att_ref, q_ref, k_ref, v_ref, prob_ref, sq_ref, sk_ref = refs[count:]
    width = w_ref.shape[1] // 3
    qkv = jnp.concatenate(
        [jnp.dot(p[...], w_ref[...], preferred_element_type=F32) for p in pieces], 0
    )
    q, sq = normalize(qkv[:, :width])
    k, sk = normalize(qkv[:, width : 2 * width])
    v = qkv[:, 2 * width :]
    weights = jnp.exp(exact(q, k, NT) * width ** (-0.5))
    probs = weights / jnp.sum(weights, -1, keepdims=True)
    att_ref[...] = exact(probs, v, NN).T.astype(BF16)
    q_ref[...] = q
    k_ref[...] = k
    v_ref[...] = v
    prob_ref[...] = probs
    sq_ref[...] = jnp.broadcast_to(sq, q.shape)
    sk_ref[...] = jnp.broadcast_to(sk, k.shape)


def backward_kernel(*refs, count):
    pieces = refs[:count]
    w_ref, q_ref, k_ref, v_ref, prob_ref, sq_ref, sk_ref, out_ref = refs[count:]
    width = w_ref.shape[0]
    cot = jnp.concatenate([piece[...] for piece in pieces], 0)
    d_att = lax.dot_general(cot, w_ref[...], NT, preferred_element_type=F32)
    q, k, v, probs = q_ref[...], k_ref[...], v_ref[...], prob_ref[...]
    d_value = exact(probs, d_att, TM)
    d_probs = exact(d_att, v, NT)
    inner = jnp.sum(d_probs * probs, -1, keepdims=True)
    d_scores = probs * (d_probs - inner) * width ** (-0.5)
    d_q = normalize_back(exact(d_scores, k, NN), q, sq_ref[...])
    d_k = normalize_back(exact(d_scores, q, TM), k, sk_ref[...])
    out_ref[:width, :] = d_q.T.astype(BF16)
    out_ref[width : 2 * width, :] = d_k.T.astype(BF16)
    out_ref[2 * width :, :] = d_value.T.astype(BF16)


def terms_kernel(*refs, counts, blocks):
    place_ref, refs = refs[0], refs[1:]
    normed, pieces = refs[: counts[0]], refs[counts[0] : sum(counts)]
    d_ref, att_ref, out_ref = refs[sum(counts) :]
    far, near, width = blocks
    core, here, zh = place_ref[0], place_ref[1], place_ref[2]
    d_all, att = d_ref[...], att_ref[...]
    split = d_all.shape[0]
    for slot, distance in enumerate(ORDER):
        y = lax.rem(here + distance + near, near)
        cols = [
            pl.ds(pl.multiple_of(((z * near + y) * 2 + core) * width, width), width)
            for z in (1 - zh, zh)
        ]
        rhs = jnp.concatenate([jnp.concatenate([p[:, c] for p in normed], 0) for c in cols], 1)
        cot = jnp.concatenate([jnp.concatenate([p[:, c] for p in pieces], 0) for c in cols], 1)
        top = jnp.dot(d_all, rhs, preferred_element_type=F32)
        low = jnp.dot(att, cot, preferred_element_type=F32)
        for i in range(far):
            out_ref[slot * far + i, :split, :] = top[:, i * width : (i + 1) * width].astype(BF16)
            out_ref[slot * far + i, split:, :] = low[:, i * width : (i + 1) * width].astype(BF16)


def first_kernel(own_ref, theirs_ref, up_ref, down_ref):
    for at, out_ref in enumerate((up_ref, down_ref)):
        out_ref[...] = (own_ref[at, :, :].astype(F32) + theirs_ref[at, :, :].astype(F32)).astype(BF16)


def sum_kernel(own_ref, theirs_ref, came_ref, out_ref, *, at, half):
    for i in range(2):
        total = own_ref[at + i, :, :].astype(F32) + theirs_ref[at + i, :, :].astype(F32)
        if half is None:
            total = total + came_ref[i, :, :].astype(F32)
        elif half == i:
            total = total + came_ref[...].astype(F32)
        out_ref[i, :, :] = total.astype(BF16)


def away_kernel(own_ref, theirs_ref, up_ref, down_ref, out_ref, *, at):
    total = own_ref[at, :, :].astype(F32) + theirs_ref[at, :, :].astype(F32)
    for ref in (up_ref, down_ref):
        total = total + ref[0, :, :].astype(F32)
    out_ref[...] = total.astype(BF16)


def finish_kernel(own_ref, theirs_ref, up_ref, down_ref, other_ref, qkv_ref, out_ref, *, at):
    both = own_ref[at, :, :].astype(F32) + theirs_ref[at, :, :].astype(F32)
    for ref in (up_ref, down_ref):
        both = both + ref[1, :, :].astype(F32)
    both = both + other_ref[...].astype(F32)
    split = qkv_ref.shape[-1]
    qkv_ref[:, 0, :] = both[:split].T
    out_ref[0, :, :] = both[split:]


def swap(n, s):
    return [(i, i ^ s) for i in range(n)]


def turn(n, s):
    return [(i, (i + s) % n) for i in range(n)]


def after(value, *done):
    return lax.optimization_barrier((value, *done))[0]


def normalized(*pieces):
    rows = sum(p.shape[0] for p in pieces)
    return pl.pallas_call(
        normalize_kernel,
        out_shape=jax.ShapeDtypeStruct((rows, pieces[0].shape[1]), BF16),
        in_specs=[VMEM] * len(pieces),
        out_specs=VMEM,
        compiler_params=PARAMS,
    )(*pieces)


def gather(tokens, cotangent, n_z, n_x):
    up, down = turn(n_x, 1), turn(n_x, -1)

    def join(*rows):
        return lax.optimization_barrier(jnp.concatenate(rows, 0))

    def within(rows):
        return [lax.ppermute(rows, "zl", swap(n_z, s)) for s in (2, 3, 1)]

    t_other = lax.ppermute(tokens, "zl", swap(n_z, 4))
    t = join(tokens, t_other)
    t_near = within(t)
    c = join(cotangent, lax.ppermute(after(cotangent, t), "zl", swap(n_z, 4)))
    t = join(t, *t_near)
    t_left = lax.ppermute(t, "x", up)
    t_right = lax.ppermute(t, "x", down)
    normed = normalized(t)
    c_near = within(after(c, normed))
    c = join(after(c, t_left, t_right), *c_near)
    t_far = lax.ppermute(t_left, "x", up)
    c_right = lax.ppermute(c, "x", down)
    c_left = lax.ppermute(c, "x", up)
    rest = normalized(t_left, t_right, t_far)
    c_far = lax.ppermute(after(c_right, rest), "x", down)
    return [normed, rest], [c, c_left, c_right, c_far]


def local(sizes, tokens, cotangent, w_qkv, w_out):
    far, near, cores, n_z, n_x = sizes
    w_head = w_qkv[:, 0, :]
    w_back = w_out[0]
    model, width = w_head.shape[0], w_back.shape[0]
    normed, c_pieces = gather(tokens, cotangent, n_z, n_x)
    total = sum(p.shape[0] for p in normed)
    small = jax.ShapeDtypeStruct((total, width), F32)
    att, *saved = pl.pallas_call(
        functools.partial(forward_kernel, count=len(normed)),
        out_shape=[
            jax.ShapeDtypeStruct((width, total), BF16),
            small,
            small,
            small,
            jax.ShapeDtypeStruct((total, total), F32),
            small,
            small,
        ],
        in_specs=[VMEM] * (len(normed) + 1),
        out_specs=[VMEM] * 7,
        compiler_params=PARAMS,
    )(*normed, w_head)
    d_qkv = pl.pallas_call(
        functools.partial(backward_kernel, count=len(c_pieces)),
        out_shape=jax.ShapeDtypeStruct((3 * width, total), BF16),
        in_specs=[VMEM] * (len(c_pieces) + 7),
        out_specs=VMEM,
        compiler_params=PARAMS,
    )(*c_pieces, w_back, *saved)
    blocks = (far, near, model // (far * near * cores))
    one = jax.ShapeDtypeStruct((4 * width, blocks[2]), BF16)
    here = lax.axis_index("y").astype(jnp.int32)
    core = lax.axis_index("c").astype(jnp.int32)
    zh = lax.axis_index("zh").astype(jnp.int32)

    def terms(core):
        return pl.pallas_call(
            functools.partial(
                terms_kernel, counts=(len(normed), len(c_pieces)), blocks=blocks
            ),
            out_shape=jax.ShapeDtypeStruct((far * near, *one.shape), BF16),
            in_specs=[SMEM] + [VMEM] * (len(normed) + len(c_pieces) + 2),
            out_specs=VMEM,
            compiler_params=PARAMS,
        )(jnp.stack([core, here, zh]), *normed, *c_pieces, d_qkv, att)

    theirs = lax.ppermute(terms(1 - core), "c", swap(cores, 1))
    mine = terms(core)

    two = jax.ShapeDtypeStruct((far, *one.shape), BF16)

    def call(kernel, shapes, *came):
        return pl.pallas_call(
            kernel,
            out_shape=shapes,
            in_specs=[VMEM] * (2 + len(came)),
            out_specs=[VMEM] * len(shapes),
            compiler_params=PARAMS,
        )(mine, theirs, *came)

    goes = list(call(first_kernel, [one, one]))
    for distance in (3, 2, 1, 0):
        goes = [lax.ppermute(m, "y", turn(near, way)) for m, way in zip(goes, (1, -1))]
        if distance == 0:
            break
        for i, way in enumerate((1, -1)):
            at = ORDER.index(distance * way) * far
            half = i if distance == 3 else None
            (goes[i],) = call(functools.partial(sum_kernel, at=at, half=half), [two], goes[i])
    at = ORDER.index(0) * far
    (away,) = call(functools.partial(away_kernel, at=at), [one], *goes)
    other = lax.ppermute(away, "zh", swap(far, 1))
    return pl.pallas_call(
        functools.partial(finish_kernel, at=at + 1),
        out_shape=[
            jax.ShapeDtypeStruct((blocks[2], 1, 3 * width), F32),
            jax.ShapeDtypeStruct((1, width, blocks[2]), F32),
        ],
        in_specs=[VMEM] * 5,
        out_specs=[VMEM] * 2,
        compiler_params=PARAMS,
    )(mine, theirs, *goes, other)


def solution(mesh):
    sizes = (2, mesh.shape["dp"] // 4, 2, mesh.shape["mp"] // 4, 4)
    fine = Mesh(mesh.devices.reshape(sizes), ("zh", "y", "c", "zl", "x"))
    dp, mp = ("zh", "y", "c"), ("zl", "x")
    in_specs = (P(dp + mp, None), P(dp + mp, None), P(None, mp, None), P(mp, None, None))
    out_specs = (P(dp, mp, None), P(mp, None, dp))
    return jax.shard_map(
        functools.partial(local, sizes),
        mesh=fine,
        in_specs=in_specs,
        out_specs=out_specs,
        check_vma=False,
    )
```

```python
import functools

import jax
import jax.numpy as jnp
from jax import lax
from jax.experimental import pallas as pl
from jax.experimental.pallas import tpu as pltpu
from jax.sharding import Mesh
from jax.sharding import PartitionSpec as P

HIGHEST = lax.Precision.HIGHEST
BF16 = jnp.bfloat16
F32 = jnp.float32
EPS = 1e-6
TM = (((0,), (0,)), ((), ()))
NT = (((1,), (1,)), ((), ()))
NN = (((1,), (0,)), ((), ()))
VMEM = pl.BlockSpec(memory_space=pltpu.VMEM)
SMEM = pl.BlockSpec(memory_space=pltpu.SMEM)
ORDER = (4, 3, -3, 2, -2, 1, -1, 0)
PARAMS = pltpu.CompilerParams(vmem_limit_bytes=16 * 1024 * 1024)


def normalize(values):
    centred = values - jnp.mean(values, -1, keepdims=True)
    spread = lax.rsqrt(jnp.mean(centred * centred, -1, keepdims=True) + EPS)
    return centred * spread, spread


def normalize_back(grad, normed, spread):
    inner = jnp.mean(grad * normed, -1, keepdims=True)
    return spread * (grad - jnp.mean(grad, -1, keepdims=True) - normed * inner)


def exact(a, b, dims):
    return lax.dot_general(a, b, dims, precision=HIGHEST, preferred_element_type=F32)


def normalize_rows(piece, normed_ref, at, count):
    step = 16

    def body(i, carry):
        x = piece[pl.ds(pl.multiple_of(i * step, step), step), :].astype(F32)
        centred = x - jnp.mean(x, -1, keepdims=True)
        spread = lax.rsqrt(jnp.mean(centred * centred, -1, keepdims=True) + EPS)
        rows = pl.ds(pl.multiple_of(at + i * step, step), step)
        normed_ref[rows, :] = (centred * spread).astype(BF16)
        return carry

    lax.fori_loop(0, count // step, body, 0)


def normalize_kernel(*refs):
    normed_ref, at = refs[-1], 0
    for piece in refs[:-1]:
        normalize_rows(piece, normed_ref, at, piece.shape[0])
        at += piece.shape[0]


def forward_kernel(*refs, count):
    pieces = refs[:count]
    w_ref, att_ref, q_ref, k_ref, v_ref, prob_ref, sq_ref, sk_ref = refs[count:]
    width = w_ref.shape[1] // 3
    qkv = jnp.concatenate(
        [jnp.dot(p[...], w_ref[...], preferred_element_type=F32) for p in pieces], 0
    )
    q, sq = normalize(qkv[:, :width])
    k, sk = normalize(qkv[:, width : 2 * width])
    v = qkv[:, 2 * width :]
    weights = jnp.exp(exact(q, k, NT) * width ** (-0.5))
    probs = weights / jnp.sum(weights, -1, keepdims=True)
    att_ref[...] = exact(probs, v, NN).T.astype(BF16)
    q_ref[...] = q
    k_ref[...] = k
    v_ref[...] = v
    prob_ref[...] = probs
    sq_ref[...] = jnp.broadcast_to(sq, q.shape)
    sk_ref[...] = jnp.broadcast_to(sk, k.shape)


def backward_kernel(*refs, count):
    pieces = refs[:count]
    w_ref, q_ref, k_ref, v_ref, prob_ref, sq_ref, sk_ref, out_ref = refs[count:]
    width = w_ref.shape[0]
    cot = jnp.concatenate([piece[...] for piece in pieces], 0)
    d_att = lax.dot_general(cot, w_ref[...], NT, preferred_element_type=F32)
    q, k, v, probs = q_ref[...], k_ref[...], v_ref[...], prob_ref[...]
    d_value = exact(probs, d_att, TM)
    d_probs = exact(d_att, v, NT)
    inner = jnp.sum(d_probs * probs, -1, keepdims=True)
    d_scores = probs * (d_probs - inner) * width ** (-0.5)
    d_q = normalize_back(exact(d_scores, k, NN), q, sq_ref[...])
    d_k = normalize_back(exact(d_scores, q, TM), k, sk_ref[...])
    out_ref[:width, :] = d_q.T.astype(BF16)
    out_ref[width : 2 * width, :] = d_k.T.astype(BF16)
    out_ref[2 * width :, :] = d_value.T.astype(BF16)


def terms_kernel(*refs, counts, blocks):
    place_ref, refs = refs[0], refs[1:]
    normed, pieces = refs[: counts[0]], refs[counts[0] : sum(counts)]
    d_ref, att_ref, out_ref = refs[sum(counts) :]
    far, near, width = blocks
    core, here, zh = place_ref[0], place_ref[1], place_ref[2]
    d_all, att = d_ref[...], att_ref[...]
    split = d_all.shape[0]
    for slot, distance in enumerate(ORDER):
        y = lax.rem(here + distance * (1 - 2 * core) + near, near)
        cols = [
            pl.ds(pl.multiple_of(((z * near + y) * 2 + core) * width, width), width)
            for z in (1 - zh, zh)
        ]
        rhs = jnp.concatenate([jnp.concatenate([p[:, c] for p in normed], 0) for c in cols], 1)
        cot = jnp.concatenate([jnp.concatenate([p[:, c] for p in pieces], 0) for c in cols], 1)
        top = jnp.dot(d_all, rhs, preferred_element_type=F32)
        low = jnp.dot(att, cot, preferred_element_type=F32)
        for i in range(far):
            out_ref[slot * far + i, :split, :] = top[:, i * width : (i + 1) * width].astype(BF16)
            out_ref[slot * far + i, split:, :] = low[:, i * width : (i + 1) * width].astype(BF16)


def first_kernel(own_ref, theirs_ref, up_ref, down_ref):
    for at, out_ref in enumerate((up_ref, down_ref)):
        out_ref[...] = (own_ref[at, :, :].astype(F32) + theirs_ref[at, :, :].astype(F32)).astype(BF16)


def sum_kernel(own_ref, theirs_ref, came_ref, out_ref, *, at, half):
    for i in range(2):
        total = own_ref[at + i, :, :].astype(F32) + theirs_ref[at + i, :, :].astype(F32)
        if half is None:
            total = total + came_ref[i, :, :].astype(F32)
        elif half == i:
            total = total + came_ref[...].astype(F32)
        out_ref[i, :, :] = total.astype(BF16)


def away_kernel(own_ref, theirs_ref, up_ref, down_ref, out_ref, *, at):
    total = own_ref[at, :, :].astype(F32) + theirs_ref[at, :, :].astype(F32)
    for ref in (up_ref, down_ref):
        total = total + ref[0, :, :].astype(F32)
    out_ref[...] = total.astype(BF16)


def finish_kernel(own_ref, theirs_ref, up_ref, down_ref, other_ref, qkv_ref, out_ref, *, at):
    both = own_ref[at, :, :].astype(F32) + theirs_ref[at, :, :].astype(F32)
    for ref in (up_ref, down_ref):
        both = both + ref[1, :, :].astype(F32)
    both = both + other_ref[...].astype(F32)
    split = qkv_ref.shape[-1]
    qkv_ref[:, 0, :] = both[:split].T
    out_ref[0, :, :] = both[split:]


def swap(n, s):
    return [(i, i ^ s) for i in range(n)]


def after(value, *done):
    return lax.optimization_barrier((value, *done))[0]


def normalized(*pieces):
    rows = sum(p.shape[0] for p in pieces)
    return pl.pallas_call(
        normalize_kernel,
        out_shape=jax.ShapeDtypeStruct((rows, pieces[0].shape[1]), BF16),
        in_specs=[VMEM] * len(pieces),
        out_specs=VMEM,
        compiler_params=PARAMS,
    )(*pieces)


def gather(tokens, cotangent, n_z, n_x):
    def join(*rows):
        return lax.optimization_barrier(jnp.concatenate(rows, 0))

    def round_x(rows, way):
        pairs = [
            (c * n_x + x, c * n_x + (x + way * (1 - 2 * c)) % n_x) for c in range(2) for x in range(n_x)
        ]
        return lax.ppermute(rows, ("c", "x"), pairs)

    def within(rows):
        return [lax.ppermute(rows, "zl", swap(n_z, s)) for s in (2, 3, 1)]

    t_other = lax.ppermute(tokens, "zl", swap(n_z, 4))
    t = join(tokens, t_other)
    t_near = within(t)
    c = join(cotangent, lax.ppermute(after(cotangent, t), "zl", swap(n_z, 4)))
    t = join(t, *t_near)
    t_one = round_x(t, 1)
    t_two = round_x(t, -1)
    normed = normalized(t)
    c_near = within(after(c, normed))
    c = join(after(c, t_one, t_two), *c_near)
    t_far = round_x(t_two, -1)
    c_one = round_x(c, 1)
    c_two = round_x(c, -1)
    rest = normalized(t_one, t_two, t_far)
    c_far = round_x(after(c_one, rest), 1)
    return [normed, rest], [c, c_one, c_two, c_far]


def local(sizes, tokens, cotangent, w_qkv, w_out):
    far, near, cores, n_z, n_x = sizes
    w_head = w_qkv[:, 0, :]
    w_back = w_out[0]
    model, width = w_head.shape[0], w_back.shape[0]
    normed, c_pieces = gather(tokens, cotangent, n_z, n_x)
    total = sum(p.shape[0] for p in normed)
    small = jax.ShapeDtypeStruct((total, width), F32)
    att, *saved = pl.pallas_call(
        functools.partial(forward_kernel, count=len(normed)),
        out_shape=[
            jax.ShapeDtypeStruct((width, total), BF16),
            small,
            small,
            small,
            jax.ShapeDtypeStruct((total, total), F32),
            small,
            small,
        ],
        in_specs=[VMEM] * (len(normed) + 1),
        out_specs=[VMEM] * 7,
        compiler_params=PARAMS,
    )(*normed, w_head)
    d_qkv = pl.pallas_call(
        functools.partial(backward_kernel, count=len(c_pieces)),
        out_shape=jax.ShapeDtypeStruct((3 * width, total), BF16),
        in_specs=[VMEM] * (len(c_pieces) + 7),
        out_specs=VMEM,
        compiler_params=PARAMS,
    )(*c_pieces, w_back, *saved)
    blocks = (far, near, model // (far * near * cores))
    one = jax.ShapeDtypeStruct((4 * width, blocks[2]), BF16)
    here = lax.axis_index("y").astype(jnp.int32)
    core = lax.axis_index("c").astype(jnp.int32)
    zh = lax.axis_index("zh").astype(jnp.int32)

    def terms(core):
        return pl.pallas_call(
            functools.partial(
                terms_kernel, counts=(len(normed), len(c_pieces)), blocks=blocks
            ),
            out_shape=jax.ShapeDtypeStruct((far * near, *one.shape), BF16),
            in_specs=[SMEM] + [VMEM] * (len(normed) + len(c_pieces) + 2),
            out_specs=VMEM,
            compiler_params=PARAMS,
        )(jnp.stack([core, here, zh]), *normed, *c_pieces, d_qkv, att)

    theirs = lax.ppermute(terms(1 - core), "c", swap(cores, 1))
    mine = terms(core)

    two = jax.ShapeDtypeStruct((far, *one.shape), BF16)

    def call(kernel, shapes, *came):
        return pl.pallas_call(
            kernel,
            out_shape=shapes,
            in_specs=[VMEM] * (2 + len(came)),
            out_specs=[VMEM] * len(shapes),
            compiler_params=PARAMS,
        )(mine, theirs, *came)

    def round_y(block, way):
        pairs = [
            (y * 2 + c, (y + way * (1 - 2 * c)) % near * 2 + c) for y in range(near) for c in range(2)
        ]
        return lax.ppermute(block, ("y", "c"), pairs)

    goes = list(call(first_kernel, [one, one]))
    for distance in (3, 2, 1, 0):
        goes = [round_y(m, way) for m, way in zip(goes, (1, -1))]
        if distance == 0:
            break
        for i, way in enumerate((1, -1)):
            at = ORDER.index(distance * way) * far
            half = i if distance == 3 else None
            (goes[i],) = call(functools.partial(sum_kernel, at=at, half=half), [two], goes[i])
    at = ORDER.index(0) * far
    (away,) = call(functools.partial(away_kernel, at=at), [one], *goes)
    other = lax.ppermute(away, "zh", swap(far, 1))
    return pl.pallas_call(
        functools.partial(finish_kernel, at=at + 1),
        out_shape=[
            jax.ShapeDtypeStruct((blocks[2], 1, 3 * width), F32),
            jax.ShapeDtypeStruct((1, width, blocks[2]), F32),
        ],
        in_specs=[VMEM] * 5,
        out_specs=[VMEM] * 2,
        compiler_params=PARAMS,
    )(mine, theirs, *goes, other)


def solution(mesh):
    sizes = (2, mesh.shape["dp"] // 4, 2, mesh.shape["mp"] // 4, 4)
    fine = Mesh(mesh.devices.reshape(sizes), ("zh", "y", "c", "zl", "x"))
    dp, mp = ("zh", "y", "c"), ("zl", "x")
    in_specs = (P(dp + mp, None), P(dp + mp, None), P(None, mp, None), P(mp, None, None))
    out_specs = (P(dp, mp, None), P(mp, None, dp))
    return jax.shard_map(
        functools.partial(local, sizes),
        mesh=fine,
        in_specs=in_specs,
        out_specs=out_specs,
        check_vma=False,
    )
```

```python
import functools

import jax
import jax.numpy as jnp
from jax import lax
from jax.experimental import pallas as pl
from jax.experimental.pallas import tpu as pltpu
from jax.sharding import Mesh
from jax.sharding import PartitionSpec as P

HIGHEST = lax.Precision.HIGHEST
BF16 = jnp.bfloat16
F32 = jnp.float32
EPS = 1e-6
TM = (((0,), (0,)), ((), ()))
NT = (((1,), (1,)), ((), ()))
NN = (((1,), (0,)), ((), ()))
VMEM = pl.BlockSpec(memory_space=pltpu.VMEM)
SMEM = pl.BlockSpec(memory_space=pltpu.SMEM)
ORDER = (4, 3, -3, 2, -2, 1, -1, 0)
PARAMS = pltpu.CompilerParams(vmem_limit_bytes=16 * 1024 * 1024)


def normalize(values):
    centred = values - jnp.mean(values, -1, keepdims=True)
    spread = lax.rsqrt(jnp.mean(centred * centred, -1, keepdims=True) + EPS)
    return centred * spread, spread


def normalize_back(grad, normed, spread):
    inner = jnp.mean(grad * normed, -1, keepdims=True)
    return spread * (grad - jnp.mean(grad, -1, keepdims=True) - normed * inner)


def exact(a, b, dims):
    return lax.dot_general(a, b, dims, precision=HIGHEST, preferred_element_type=F32)


def normalize_rows(piece, normed_ref, at, count):
    step = 16

    def body(i, carry):
        x = piece[pl.ds(pl.multiple_of(i * step, step), step), :].astype(F32)
        centred = x - jnp.mean(x, -1, keepdims=True)
        spread = lax.rsqrt(jnp.mean(centred * centred, -1, keepdims=True) + EPS)
        rows = pl.ds(pl.multiple_of(at + i * step, step), step)
        normed_ref[rows, :] = (centred * spread).astype(BF16)
        return carry

    lax.fori_loop(0, count // step, body, 0)


def normalize_kernel(*refs):
    normed_ref, at = refs[-1], 0
    for piece in refs[:-1]:
        normalize_rows(piece, normed_ref, at, piece.shape[0])
        at += piece.shape[0]


def forward_kernel(*refs, count):
    pieces = refs[:count]
    w_ref, att_ref, q_ref, k_ref, v_ref, prob_ref, sq_ref, sk_ref = refs[count:]
    width = w_ref.shape[1] // 3
    qkv = jnp.concatenate(
        [jnp.dot(p[...], w_ref[...], preferred_element_type=F32) for p in pieces], 0
    )
    q, sq = normalize(qkv[:, :width])
    k, sk = normalize(qkv[:, width : 2 * width])
    v = qkv[:, 2 * width :]
    weights = jnp.exp(exact(q, k, NT) * width ** (-0.5))
    probs = weights / jnp.sum(weights, -1, keepdims=True)
    att_ref[...] = exact(probs, v, NN).T.astype(BF16)
    q_ref[...] = q
    k_ref[...] = k
    v_ref[...] = v
    prob_ref[...] = probs
    sq_ref[...] = jnp.broadcast_to(sq, q.shape)
    sk_ref[...] = jnp.broadcast_to(sk, k.shape)


def backward_kernel(*refs, count):
    pieces = refs[:count]
    w_ref, q_ref, k_ref, v_ref, prob_ref, sq_ref, sk_ref, out_ref = refs[count:]
    width = w_ref.shape[0]
    cot = jnp.concatenate([piece[...] for piece in pieces], 0)
    d_att = lax.dot_general(cot, w_ref[...], NT, preferred_element_type=F32)
    q, k, v, probs = q_ref[...], k_ref[...], v_ref[...], prob_ref[...]
    d_value = exact(probs, d_att, TM)
    d_probs = exact(d_att, v, NT)
    inner = jnp.sum(d_probs * probs, -1, keepdims=True)
    d_scores = probs * (d_probs - inner) * width ** (-0.5)
    d_q = normalize_back(exact(d_scores, k, NN), q, sq_ref[...])
    d_k = normalize_back(exact(d_scores, q, TM), k, sk_ref[...])
    out_ref[:width, :] = d_q.T.astype(BF16)
    out_ref[width : 2 * width, :] = d_k.T.astype(BF16)
    out_ref[2 * width :, :] = d_value.T.astype(BF16)


def terms_kernel(*refs, counts, blocks):
    place_ref, refs = refs[0], refs[1:]
    normed, pieces = refs[: counts[0]], refs[counts[0] : sum(counts)]
    d_ref, att_ref, out_ref = refs[sum(counts) :]
    far, near, width = blocks
    core, here, zh = place_ref[0], place_ref[1], place_ref[2]
    d_all, att = d_ref[...], att_ref[...]
    split = d_all.shape[0]
    for slot, distance in enumerate(ORDER):
        y = lax.rem(here + distance + near, near)
        cols = [
            pl.ds(pl.multiple_of(((z * near + y) * 2 + core) * width, width), width)
            for z in (1 - zh, zh)
        ]
        rhs = jnp.concatenate([jnp.concatenate([p[:, c] for p in normed], 0) for c in cols], 1)
        cot = jnp.concatenate([jnp.concatenate([p[:, c] for p in pieces], 0) for c in cols], 1)
        top = jnp.dot(d_all, rhs, preferred_element_type=F32)
        low = jnp.dot(att, cot, preferred_element_type=F32)
        for i in range(far):
            out_ref[slot * far + i, :split, :] = top[:, i * width : (i + 1) * width].astype(BF16)
            out_ref[slot * far + i, split:, :] = low[:, i * width : (i + 1) * width].astype(BF16)


def first_kernel(own_ref, theirs_ref, up_ref, down_ref):
    for at, out_ref in enumerate((up_ref, down_ref)):
        out_ref[...] = (own_ref[at, :, :].astype(F32) + theirs_ref[at, :, :].astype(F32)).astype(BF16)


def sum_kernel(own_ref, theirs_ref, came_ref, out_ref, *, at, half):
    for i in range(2):
        total = own_ref[at + i, :, :].astype(F32) + theirs_ref[at + i, :, :].astype(F32)
        if half is None:
            total = total + came_ref[i, :, :].astype(F32)
        elif half == i:
            total = total + came_ref[...].astype(F32)
        out_ref[i, :, :] = total.astype(BF16)


def away_kernel(own_ref, theirs_ref, up_ref, down_ref, out_ref, *, at):
    total = own_ref[at, :, :].astype(F32) + theirs_ref[at, :, :].astype(F32)
    for ref in (up_ref, down_ref):
        total = total + ref[0, :, :].astype(F32)
    out_ref[...] = total.astype(BF16)


def finish_kernel(own_ref, theirs_ref, up_ref, down_ref, other_ref, qkv_ref, out_ref, *, at):
    both = own_ref[at, :, :].astype(F32) + theirs_ref[at, :, :].astype(F32)
    for ref in (up_ref, down_ref):
        both = both + ref[1, :, :].astype(F32)
    both = both + other_ref[...].astype(F32)
    split = qkv_ref.shape[-1]
    qkv_ref[:, 0, :] = both[:split].T
    out_ref[0, :, :] = both[split:]


def swap(n, s):
    return [(i, i ^ s) for i in range(n)]


def turn(n, s):
    return [(i, (i + s) % n) for i in range(n)]


def after(value, *done):
    return lax.optimization_barrier((value, *done))[0]


def normalized(*pieces):
    rows = sum(p.shape[0] for p in pieces)
    return pl.pallas_call(
        normalize_kernel,
        out_shape=jax.ShapeDtypeStruct((rows, pieces[0].shape[1]), BF16),
        in_specs=[VMEM] * len(pieces),
        out_specs=VMEM,
        compiler_params=PARAMS,
    )(*pieces)


def gather(tokens, cotangent, n_z, n_x):
    up, down = turn(n_x, 1), turn(n_x, -1)

    def join(*rows):
        return lax.optimization_barrier(jnp.concatenate(rows, 0))

    def within(rows):
        return [lax.ppermute(rows, "zl", swap(n_z, s)) for s in (2, 3, 1)]

    t_other = lax.ppermute(tokens, "zl", swap(n_z, 4))
    t = join(tokens, t_other)
    t_near = within(t)
    c = join(cotangent, lax.ppermute(cotangent, "zl", swap(n_z, 4)))
    t = join(t, *t_near)
    t_left = lax.ppermute(t, "x", up)
    t_right = lax.ppermute(t, "x", down)
    normed = normalized(t)
    c_near = within(c)
    c = join(c, *c_near)
    t_far = lax.ppermute(t_left, "x", up)
    c_right = lax.ppermute(c, "x", down)
    c_left = lax.ppermute(after(c, t_left), "x", up)
    rest = normalized(t_left, t_right, t_far)
    c_far = lax.ppermute(c_right, "x", down)
    return [normed, rest], [c, c_left, c_right, c_far]


def local(sizes, tokens, cotangent, w_qkv, w_out):
    far, near, cores, n_z, n_x = sizes
    w_head = w_qkv[:, 0, :]
    w_back = w_out[0]
    model, width = w_head.shape[0], w_back.shape[0]
    normed, c_pieces = gather(tokens, cotangent, n_z, n_x)
    total = sum(p.shape[0] for p in normed)
    small = jax.ShapeDtypeStruct((total, width), F32)
    att, *saved = pl.pallas_call(
        functools.partial(forward_kernel, count=len(normed)),
        out_shape=[
            jax.ShapeDtypeStruct((width, total), BF16),
            small,
            small,
            small,
            jax.ShapeDtypeStruct((total, total), F32),
            small,
            small,
        ],
        in_specs=[VMEM] * (len(normed) + 1),
        out_specs=[VMEM] * 7,
        compiler_params=PARAMS,
    )(*normed, w_head)
    d_qkv = pl.pallas_call(
        functools.partial(backward_kernel, count=len(c_pieces)),
        out_shape=jax.ShapeDtypeStruct((3 * width, total), BF16),
        in_specs=[VMEM] * (len(c_pieces) + 7),
        out_specs=VMEM,
        compiler_params=PARAMS,
    )(*c_pieces, w_back, *saved)
    blocks = (far, near, model // (far * near * cores))
    one = jax.ShapeDtypeStruct((4 * width, blocks[2]), BF16)
    here = lax.axis_index("y").astype(jnp.int32)
    core = lax.axis_index("c").astype(jnp.int32)
    zh = lax.axis_index("zh").astype(jnp.int32)

    def terms(core):
        return pl.pallas_call(
            functools.partial(
                terms_kernel, counts=(len(normed), len(c_pieces)), blocks=blocks
            ),
            out_shape=jax.ShapeDtypeStruct((far * near, *one.shape), BF16),
            in_specs=[SMEM] + [VMEM] * (len(normed) + len(c_pieces) + 2),
            out_specs=VMEM,
            compiler_params=PARAMS,
        )(jnp.stack([core, here, zh]), *normed, *c_pieces, d_qkv, att)

    theirs = lax.ppermute(terms(1 - core), "c", swap(cores, 1))
    mine = terms(core)

    two = jax.ShapeDtypeStruct((far, *one.shape), BF16)

    def call(kernel, shapes, *came):
        return pl.pallas_call(
            kernel,
            out_shape=shapes,
            in_specs=[VMEM] * (2 + len(came)),
            out_specs=[VMEM] * len(shapes),
            compiler_params=PARAMS,
        )(mine, theirs, *came)

    goes = list(call(first_kernel, [one, one]))
    for distance in (3, 2, 1, 0):
        goes = [lax.ppermute(m, "y", turn(near, way)) for m, way in zip(goes, (1, -1))]
        if distance == 0:
            break
        for i, way in enumerate((1, -1)):
            at = ORDER.index(distance * way) * far
            half = i if distance == 3 else None
            (goes[i],) = call(functools.partial(sum_kernel, at=at, half=half), [two], goes[i])
    at = ORDER.index(0) * far
    (away,) = call(functools.partial(away_kernel, at=at), [one], *goes)
    other = lax.ppermute(away, "zh", swap(far, 1))
    return pl.pallas_call(
        functools.partial(finish_kernel, at=at + 1),
        out_shape=[
            jax.ShapeDtypeStruct((blocks[2], 1, 3 * width), F32),
            jax.ShapeDtypeStruct((1, width, blocks[2]), F32),
        ],
        in_specs=[VMEM] * 5,
        out_specs=[VMEM] * 2,
        compiler_params=PARAMS,
    )(mine, theirs, *goes, other)


def solution(mesh):
    sizes = (2, mesh.shape["dp"] // 4, 2, mesh.shape["mp"] // 4, 4)
    fine = Mesh(mesh.devices.reshape(sizes), ("zh", "y", "c", "zl", "x"))
    dp, mp = ("zh", "y", "c"), ("zl", "x")
    in_specs = (P(dp + mp, None), P(dp + mp, None), P(None, mp, None), P(mp, None, None))
    out_specs = (P(dp, mp, None), P(mp, None, dp))
    return jax.shard_map(
        functools.partial(local, sizes),
        mesh=fine,
        in_specs=in_specs,
        out_specs=out_specs,
        check_vma=False,
    )
```

```python
import functools

import jax
import jax.numpy as jnp
from jax import lax
from jax.experimental import pallas as pl
from jax.experimental.pallas import tpu as pltpu
from jax.sharding import Mesh
from jax.sharding import PartitionSpec as P

HIGHEST = lax.Precision.HIGHEST
BF16 = jnp.bfloat16
F32 = jnp.float32
EPS = 1e-6
TM = (((0,), (0,)), ((), ()))
NT = (((1,), (1,)), ((), ()))
NN = (((1,), (0,)), ((), ()))
VMEM = pl.BlockSpec(memory_space=pltpu.VMEM)
SMEM = pl.BlockSpec(memory_space=pltpu.SMEM)
ORDER = (4, 3, -3, 2, -2, 1, -1, 0)
PARAMS = pltpu.CompilerParams(vmem_limit_bytes=16 * 1024 * 1024)


def normalize(values):
    centred = values - jnp.mean(values, -1, keepdims=True)
    spread = lax.rsqrt(jnp.mean(centred * centred, -1, keepdims=True) + EPS)
    return centred * spread, spread


def normalize_back(grad, normed, spread):
    inner = jnp.mean(grad * normed, -1, keepdims=True)
    return spread * (grad - jnp.mean(grad, -1, keepdims=True) - normed * inner)


def exact(a, b, dims):
    return lax.dot_general(a, b, dims, precision=HIGHEST, preferred_element_type=F32)


def normalize_rows(piece, normed_ref, at, count):
    step = 16

    def body(i, carry):
        x = piece[pl.ds(pl.multiple_of(i * step, step), step), :].astype(F32)
        centred = x - jnp.mean(x, -1, keepdims=True)
        spread = lax.rsqrt(jnp.mean(centred * centred, -1, keepdims=True) + EPS)
        rows = pl.ds(pl.multiple_of(at + i * step, step), step)
        normed_ref[rows, :] = (centred * spread).astype(BF16)
        return carry

    lax.fori_loop(0, count // step, body, 0)


def normalize_kernel(*refs):
    normed_ref, at = refs[-1], 0
    for piece in refs[:-1]:
        normalize_rows(piece, normed_ref, at, piece.shape[0])
        at += piece.shape[0]


def forward_kernel(*refs, count):
    pieces = refs[:count]
    w_ref, att_ref, q_ref, k_ref, v_ref, prob_ref, sq_ref, sk_ref = refs[count:]
    width = w_ref.shape[1] // 3
    qkv = jnp.concatenate(
        [jnp.dot(p[...], w_ref[...], preferred_element_type=F32) for p in pieces], 0
    )
    q, sq = normalize(qkv[:, :width])
    k, sk = normalize(qkv[:, width : 2 * width])
    v = qkv[:, 2 * width :]
    weights = jnp.exp(exact(q, k, NT) * width ** (-0.5))
    probs = weights / jnp.sum(weights, -1, keepdims=True)
    att_ref[...] = exact(probs, v, NN).T.astype(BF16)
    q_ref[...] = q
    k_ref[...] = k
    v_ref[...] = v
    prob_ref[...] = probs
    sq_ref[...] = jnp.broadcast_to(sq, q.shape)
    sk_ref[...] = jnp.broadcast_to(sk, k.shape)


def backward_kernel(*refs, count):
    pieces = refs[:count]
    w_ref, q_ref, k_ref, v_ref, prob_ref, sq_ref, sk_ref, out_ref = refs[count:]
    width = w_ref.shape[0]
    cot = jnp.concatenate([piece[...] for piece in pieces], 0)
    d_att = lax.dot_general(cot, w_ref[...], NT, preferred_element_type=F32)
    q, k, v, probs = q_ref[...], k_ref[...], v_ref[...], prob_ref[...]
    d_value = exact(probs, d_att, TM)
    d_probs = exact(d_att, v, NT)
    inner = jnp.sum(d_probs * probs, -1, keepdims=True)
    d_scores = probs * (d_probs - inner) * width ** (-0.5)
    d_q = normalize_back(exact(d_scores, k, NN), q, sq_ref[...])
    d_k = normalize_back(exact(d_scores, q, TM), k, sk_ref[...])
    out_ref[:width, :] = d_q.T.astype(BF16)
    out_ref[width : 2 * width, :] = d_k.T.astype(BF16)
    out_ref[2 * width :, :] = d_value.T.astype(BF16)


def terms_kernel(*refs, counts, blocks):
    place_ref, refs = refs[0], refs[1:]
    normed, pieces = refs[: counts[0]], refs[counts[0] : sum(counts)]
    d_ref, att_ref, out_ref = refs[sum(counts) :]
    far, near, width = blocks
    core, here, zh = place_ref[0], place_ref[1], place_ref[2]
    d_all, att = d_ref[...], att_ref[...]
    split = d_all.shape[0]
    for slot, distance in enumerate(ORDER):
        y = lax.rem(here + distance + near, near)
        cols = [
            pl.ds(pl.multiple_of(((z * near + y) * 2 + core) * width, width), width)
            for z in (1 - zh, zh)
        ]
        rhs = jnp.concatenate([jnp.concatenate([p[:, c] for p in normed], 0) for c in cols], 1)
        cot = jnp.concatenate([jnp.concatenate([p[:, c] for p in pieces], 0) for c in cols], 1)
        top = jnp.dot(d_all, rhs, preferred_element_type=F32)
        low = jnp.dot(att, cot, preferred_element_type=F32)
        for i in range(far):
            out_ref[slot * far + i, :split, :] = top[:, i * width : (i + 1) * width].astype(BF16)
            out_ref[slot * far + i, split:, :] = low[:, i * width : (i + 1) * width].astype(BF16)


def first_kernel(own_ref, theirs_ref, up_ref, down_ref):
    for at, out_ref in enumerate((up_ref, down_ref)):
        out_ref[...] = (own_ref[at, :, :].astype(F32) + theirs_ref[at, :, :].astype(F32)).astype(BF16)


def sum_kernel(own_ref, theirs_ref, came_ref, out_ref, *, at, half):
    for i in range(2):
        total = own_ref[at + i, :, :].astype(F32) + theirs_ref[at + i, :, :].astype(F32)
        if half is None:
            total = total + came_ref[i, :, :].astype(F32)
        elif half == i:
            total = total + came_ref[...].astype(F32)
        out_ref[i, :, :] = total.astype(BF16)


def away_kernel(own_ref, theirs_ref, up_ref, down_ref, out_ref, *, at):
    total = own_ref[at, :, :].astype(F32) + theirs_ref[at, :, :].astype(F32)
    for ref in (up_ref, down_ref):
        total = total + ref[0, :, :].astype(F32)
    out_ref[...] = total.astype(BF16)


def finish_kernel(own_ref, theirs_ref, up_ref, down_ref, other_ref, qkv_ref, out_ref, *, at):
    both = own_ref[at, :, :].astype(F32) + theirs_ref[at, :, :].astype(F32)
    for ref in (up_ref, down_ref):
        both = both + ref[1, :, :].astype(F32)
    both = both + other_ref[...].astype(F32)
    split = qkv_ref.shape[-1]
    qkv_ref[:, 0, :] = both[:split].T
    out_ref[0, :, :] = both[split:]


def swap(n, s):
    return [(i, i ^ s) for i in range(n)]


def turn(n, s):
    return [(i, (i + s) % n) for i in range(n)]


def after(value, *done):
    return lax.optimization_barrier((value, *done))[0]


def normalized(*pieces):
    rows = sum(p.shape[0] for p in pieces)
    return pl.pallas_call(
        normalize_kernel,
        out_shape=jax.ShapeDtypeStruct((rows, pieces[0].shape[1]), BF16),
        in_specs=[VMEM] * len(pieces),
        out_specs=VMEM,
        compiler_params=PARAMS,
    )(*pieces)


def gather(tokens, cotangent, n_z, n_x):
    up, down = turn(n_x, 1), turn(n_x, -1)

    def join(*rows):
        return lax.optimization_barrier(jnp.concatenate(rows, 0))

    def within(rows):
        return [lax.ppermute(rows, "zl", swap(n_z, s)) for s in (2, 3, 1)]

    t_other = lax.ppermute(tokens, "zl", swap(n_z, 4))
    t = join(tokens, t_other)
    t_near = within(t)
    c = join(cotangent, lax.ppermute(after(cotangent, t), "zl", swap(n_z, 4)))
    t = join(t, *t_near)
    t_left = lax.ppermute(t, "x", up)
    t_right = lax.ppermute(t, "x", down)
    normed = normalized(t)
    c_near = within(c)
    c = join(c, *c_near)
    t_far = lax.ppermute(t_left, "x", up)
    c_right = lax.ppermute(c, "x", down)
    c_left = lax.ppermute(after(c, t_left), "x", up)
    left = normalized(t_left)
    rest = normalized(t_right, t_far)
    c_far = lax.ppermute(c_right, "x", down)
    return [normed, left, rest], [c, c_left, c_right, c_far]


def local(sizes, tokens, cotangent, w_qkv, w_out):
    far, near, cores, n_z, n_x = sizes
    w_head = w_qkv[:, 0, :]
    w_back = w_out[0]
    model, width = w_head.shape[0], w_back.shape[0]
    normed, c_pieces = gather(tokens, cotangent, n_z, n_x)
    total = sum(p.shape[0] for p in normed)
    small = jax.ShapeDtypeStruct((total, width), F32)
    att, *saved = pl.pallas_call(
        functools.partial(forward_kernel, count=len(normed)),
        out_shape=[
            jax.ShapeDtypeStruct((width, total), BF16),
            small,
            small,
            small,
            jax.ShapeDtypeStruct((total, total), F32),
            small,
            small,
        ],
        in_specs=[VMEM] * (len(normed) + 1),
        out_specs=[VMEM] * 7,
        compiler_params=PARAMS,
    )(*normed, w_head)
    d_qkv = pl.pallas_call(
        functools.partial(backward_kernel, count=len(c_pieces)),
        out_shape=jax.ShapeDtypeStruct((3 * width, total), BF16),
        in_specs=[VMEM] * (len(c_pieces) + 7),
        out_specs=VMEM,
        compiler_params=PARAMS,
    )(*c_pieces, w_back, *saved)
    blocks = (far, near, model // (far * near * cores))
    one = jax.ShapeDtypeStruct((4 * width, blocks[2]), BF16)
    here = lax.axis_index("y").astype(jnp.int32)
    core = lax.axis_index("c").astype(jnp.int32)
    zh = lax.axis_index("zh").astype(jnp.int32)

    def terms(core):
        return pl.pallas_call(
            functools.partial(
                terms_kernel, counts=(len(normed), len(c_pieces)), blocks=blocks
            ),
            out_shape=jax.ShapeDtypeStruct((far * near, *one.shape), BF16),
            in_specs=[SMEM] + [VMEM] * (len(normed) + len(c_pieces) + 2),
            out_specs=VMEM,
            compiler_params=PARAMS,
        )(jnp.stack([core, here, zh]), *normed, *c_pieces, d_qkv, att)

    theirs = lax.ppermute(terms(1 - core), "c", swap(cores, 1))
    mine = terms(core)

    two = jax.ShapeDtypeStruct((far, *one.shape), BF16)

    def call(kernel, shapes, *came):
        return pl.pallas_call(
            kernel,
            out_shape=shapes,
            in_specs=[VMEM] * (2 + len(came)),
            out_specs=[VMEM] * len(shapes),
            compiler_params=PARAMS,
        )(mine, theirs, *came)

    goes = list(call(first_kernel, [one, one]))
    for distance in (3, 2, 1, 0):
        goes = [lax.ppermute(m, "y", turn(near, way)) for m, way in zip(goes, (1, -1))]
        if distance == 0:
            break
        for i, way in enumerate((1, -1)):
            at = ORDER.index(distance * way) * far
            half = i if distance == 3 else None
            (goes[i],) = call(functools.partial(sum_kernel, at=at, half=half), [two], goes[i])
    at = ORDER.index(0) * far
    (away,) = call(functools.partial(away_kernel, at=at), [one], *goes)
    other = lax.ppermute(away, "zh", swap(far, 1))
    return pl.pallas_call(
        functools.partial(finish_kernel, at=at + 1),
        out_shape=[
            jax.ShapeDtypeStruct((blocks[2], 1, 3 * width), F32),
            jax.ShapeDtypeStruct((1, width, blocks[2]), F32),
        ],
        in_specs=[VMEM] * 5,
        out_specs=[VMEM] * 2,
        compiler_params=PARAMS,
    )(mine, theirs, *goes, other)


def solution(mesh):
    sizes = (2, mesh.shape["dp"] // 4, 2, mesh.shape["mp"] // 4, 4)
    fine = Mesh(mesh.devices.reshape(sizes), ("zh", "y", "c", "zl", "x"))
    dp, mp = ("zh", "y", "c"), ("zl", "x")
    in_specs = (P(dp + mp, None), P(dp + mp, None), P(None, mp, None), P(mp, None, None))
    out_specs = (P(dp, mp, None), P(mp, None, dp))
    return jax.shard_map(
        functools.partial(local, sizes),
        mesh=fine,
        in_specs=in_specs,
        out_specs=out_specs,
        check_vma=False,
    )
```

```python
import functools

import jax
import jax.numpy as jnp
from jax import lax
from jax.experimental import pallas as pl
from jax.experimental.pallas import tpu as pltpu
from jax.sharding import Mesh
from jax.sharding import PartitionSpec as P

HIGHEST = lax.Precision.HIGHEST
BF16 = jnp.bfloat16
F32 = jnp.float32
EPS = 1e-6
TM = (((0,), (0,)), ((), ()))
NT = (((1,), (1,)), ((), ()))
NN = (((1,), (0,)), ((), ()))
VMEM = pl.BlockSpec(memory_space=pltpu.VMEM)
SMEM = pl.BlockSpec(memory_space=pltpu.SMEM)
ORDER = (4, 3, -3, 2, -2, 1, -1, 0)
PARAMS = pltpu.CompilerParams(vmem_limit_bytes=16 * 1024 * 1024)


def normalize(values):
    centred = values - jnp.mean(values, -1, keepdims=True)
    spread = lax.rsqrt(jnp.mean(centred * centred, -1, keepdims=True) + EPS)
    return centred * spread, spread


def normalize_back(grad, normed, spread):
    inner = jnp.mean(grad * normed, -1, keepdims=True)
    return spread * (grad - jnp.mean(grad, -1, keepdims=True) - normed * inner)


def exact(a, b, dims):
    return lax.dot_general(a, b, dims, precision=HIGHEST, preferred_element_type=F32)


def normalize_rows(piece, normed_ref, at, count):
    step = 16

    def body(i, carry):
        x = piece[pl.ds(pl.multiple_of(i * step, step), step), :].astype(F32)
        centred = x - jnp.mean(x, -1, keepdims=True)
        spread = lax.rsqrt(jnp.mean(centred * centred, -1, keepdims=True) + EPS)
        rows = pl.ds(pl.multiple_of(at + i * step, step), step)
        normed_ref[rows, :] = (centred * spread).astype(BF16)
        return carry

    lax.fori_loop(0, count // step, body, 0)


def normalize_kernel(*refs):
    normed_ref, at = refs[-1], 0
    for piece in refs[:-1]:
        normalize_rows(piece, normed_ref, at, piece.shape[0])
        at += piece.shape[0]


def forward_kernel(*refs, count):
    pieces = refs[:count]
    w_ref, att_ref, q_ref, k_ref, v_ref, prob_ref, sq_ref, sk_ref = refs[count:]
    width = w_ref.shape[1] // 3
    qkv = jnp.concatenate(
        [jnp.dot(p[...], w_ref[...], preferred_element_type=F32) for p in pieces], 0
    )
    q, sq = normalize(qkv[:, :width])
    k, sk = normalize(qkv[:, width : 2 * width])
    v = qkv[:, 2 * width :]
    weights = jnp.exp(exact(q, k, NT) * width ** (-0.5))
    probs = weights / jnp.sum(weights, -1, keepdims=True)
    att_ref[...] = exact(probs, v, NN).T.astype(BF16)
    q_ref[...] = q
    k_ref[...] = k
    v_ref[...] = v
    prob_ref[...] = probs
    sq_ref[...] = jnp.broadcast_to(sq, q.shape)
    sk_ref[...] = jnp.broadcast_to(sk, k.shape)


def backward_kernel(*refs, count):
    pieces = refs[:count]
    w_ref, q_ref, k_ref, v_ref, prob_ref, sq_ref, sk_ref, out_ref = refs[count:]
    width = w_ref.shape[0]
    cot = jnp.concatenate([piece[...] for piece in pieces], 0)
    d_att = lax.dot_general(cot, w_ref[...], NT, preferred_element_type=F32)
    q, k, v, probs = q_ref[...], k_ref[...], v_ref[...], prob_ref[...]
    d_value = exact(probs, d_att, TM)
    d_probs = exact(d_att, v, NT)
    inner = jnp.sum(d_probs * probs, -1, keepdims=True)
    d_scores = probs * (d_probs - inner) * width ** (-0.5)
    d_q = normalize_back(exact(d_scores, k, NN), q, sq_ref[...])
    d_k = normalize_back(exact(d_scores, q, TM), k, sk_ref[...])
    out_ref[:width, :] = d_q.T.astype(BF16)
    out_ref[width : 2 * width, :] = d_k.T.astype(BF16)
    out_ref[2 * width :, :] = d_value.T.astype(BF16)


def terms_kernel(*refs, counts, blocks):
    place_ref, refs = refs[0], refs[1:]
    normed, pieces = refs[: counts[0]], refs[counts[0] : sum(counts)]
    d_ref, att_ref, out_ref = refs[sum(counts) :]
    far, near, width = blocks
    core, here, zh = place_ref[0], place_ref[1], place_ref[2]
    d_all, att = d_ref[...], att_ref[...]
    split = d_all.shape[0]
    for slot, distance in enumerate(ORDER):
        y = lax.rem(here + distance + near, near)
        cols = [
            pl.ds(pl.multiple_of(((z * near + y) * 2 + core) * width, width), width)
            for z in (1 - zh, zh)
        ]
        rhs = jnp.concatenate([jnp.concatenate([p[:, c] for p in normed], 0) for c in cols], 1)
        cot = jnp.concatenate([jnp.concatenate([p[:, c] for p in pieces], 0) for c in cols], 1)
        top = jnp.dot(d_all, rhs, preferred_element_type=F32)
        low = jnp.dot(att, cot, preferred_element_type=F32)
        for i in range(far):
            out_ref[slot * far + i, :split, :] = top[:, i * width : (i + 1) * width].astype(BF16)
            out_ref[slot * far + i, split:, :] = low[:, i * width : (i + 1) * width].astype(BF16)


def first_kernel(own_ref, theirs_ref, up_ref, down_ref, far_up_ref, far_down_ref):
    def term(at):
        return (own_ref[at, :, :].astype(F32) + theirs_ref[at, :, :].astype(F32)).astype(BF16)

    far_up_ref[...] = term(0)
    far_down_ref[...] = term(1)
    for out_ref, distance in ((up_ref, 3), (down_ref, -3)):
        for i in range(2):
            out_ref[i, :, :] = term(ORDER.index(distance) * 2 + i)


def sum_kernel(own_ref, theirs_ref, came_ref, *rest, at, half):
    *far_ref, out_ref = rest
    for i in range(2):
        total = own_ref[at + i, :, :].astype(F32) + theirs_ref[at + i, :, :].astype(F32)
        total = total + came_ref[i, :, :].astype(F32)
        if far_ref and half == i:
            total = total + far_ref[0][...].astype(F32)
        out_ref[i, :, :] = total.astype(BF16)


def away_kernel(own_ref, theirs_ref, up_ref, down_ref, out_ref, *, at):
    total = own_ref[at, :, :].astype(F32) + theirs_ref[at, :, :].astype(F32)
    for ref in (up_ref, down_ref):
        total = total + ref[0, :, :].astype(F32)
    out_ref[...] = total.astype(BF16)


def finish_kernel(own_ref, theirs_ref, up_ref, down_ref, other_ref, qkv_ref, out_ref, *, at):
    both = own_ref[at, :, :].astype(F32) + theirs_ref[at, :, :].astype(F32)
    for ref in (up_ref, down_ref):
        both = both + ref[1, :, :].astype(F32)
    both = both + other_ref[...].astype(F32)
    split = qkv_ref.shape[-1]
    qkv_ref[:, 0, :] = both[:split].T
    out_ref[0, :, :] = both[split:]


def swap(n, s):
    return [(i, i ^ s) for i in range(n)]


def turn(n, s):
    return [(i, (i + s) % n) for i in range(n)]


def after(value, *done):
    return lax.optimization_barrier((value, *done))[0]


def normalized(*pieces):
    rows = sum(p.shape[0] for p in pieces)
    return pl.pallas_call(
        normalize_kernel,
        out_shape=jax.ShapeDtypeStruct((rows, pieces[0].shape[1]), BF16),
        in_specs=[VMEM] * len(pieces),
        out_specs=VMEM,
        compiler_params=PARAMS,
    )(*pieces)


def gather(tokens, cotangent, n_z, n_x):
    up, down = turn(n_x, 1), turn(n_x, -1)

    def join(*rows):
        return lax.optimization_barrier(jnp.concatenate(rows, 0))

    def within(rows):
        return [lax.ppermute(rows, "zl", swap(n_z, s)) for s in (2, 3, 1)]

    t_other = lax.ppermute(tokens, "zl", swap(n_z, 4))
    t = join(tokens, t_other)
    t_near = within(t)
    c = join(cotangent, lax.ppermute(cotangent, "zl", swap(n_z, 4)))
    t = join(t, *t_near)
    t_left = lax.ppermute(t, "x", up)
    t_right = lax.ppermute(t, "x", down)
    normed = normalized(t)
    c_near = within(c)
    c = join(c, *c_near)
    t_far = lax.ppermute(t_left, "x", up)
    c_right = lax.ppermute(c, "x", down)
    c_left = lax.ppermute(after(c, t_left), "x", up)
    rest = normalized(t_left, t_right, t_far)
    c_far = lax.ppermute(c_right, "x", down)
    return [normed, rest], [c, c_left, c_right, c_far]


def local(sizes, tokens, cotangent, w_qkv, w_out):
    far, near, cores, n_z, n_x = sizes
    w_head = w_qkv[:, 0, :]
    w_back = w_out[0]
    model, width = w_head.shape[0], w_back.shape[0]
    normed, c_pieces = gather(tokens, cotangent, n_z, n_x)
    total = sum(p.shape[0] for p in normed)
    small = jax.ShapeDtypeStruct((total, width), F32)
    att, *saved = pl.pallas_call(
        functools.partial(forward_kernel, count=len(normed)),
        out_shape=[
            jax.ShapeDtypeStruct((width, total), BF16),
            small,
            small,
            small,
            jax.ShapeDtypeStruct((total, total), F32),
            small,
            small,
        ],
        in_specs=[VMEM] * (len(normed) + 1),
        out_specs=[VMEM] * 7,
        compiler_params=PARAMS,
    )(*normed, w_head)
    d_qkv = pl.pallas_call(
        functools.partial(backward_kernel, count=len(c_pieces)),
        out_shape=jax.ShapeDtypeStruct((3 * width, total), BF16),
        in_specs=[VMEM] * (len(c_pieces) + 7),
        out_specs=VMEM,
        compiler_params=PARAMS,
    )(*c_pieces, w_back, *saved)
    blocks = (far, near, model // (far * near * cores))
    one = jax.ShapeDtypeStruct((4 * width, blocks[2]), BF16)
    here = lax.axis_index("y").astype(jnp.int32)
    core = lax.axis_index("c").astype(jnp.int32)
    zh = lax.axis_index("zh").astype(jnp.int32)

    def terms(core):
        return pl.pallas_call(
            functools.partial(
                terms_kernel, counts=(len(normed), len(c_pieces)), blocks=blocks
            ),
            out_shape=jax.ShapeDtypeStruct((far * near, *one.shape), BF16),
            in_specs=[SMEM] + [VMEM] * (len(normed) + len(c_pieces) + 2),
            out_specs=VMEM,
            compiler_params=PARAMS,
        )(jnp.stack([core, here, zh]), *normed, *c_pieces, d_qkv, att)

    theirs = lax.ppermute(terms(1 - core), "c", swap(cores, 1))
    mine = terms(core)

    two = jax.ShapeDtypeStruct((far, *one.shape), BF16)

    def call(kernel, shapes, *came):
        return pl.pallas_call(
            kernel,
            out_shape=shapes,
            in_specs=[VMEM] * (2 + len(came)),
            out_specs=[VMEM] * len(shapes),
            compiler_params=PARAMS,
        )(mine, theirs, *came)

    *goes, far_up, far_down = call(first_kernel, [two, two, one, one])
    jumps = [[], []]
    for distance in (2, 1, 0):
        goes = [lax.ppermute(m, "y", turn(near, way)) for m, way in zip(goes, (1, -1))]
        if distance == 2:
            jumps = [
                [lax.ppermute(m, "y", turn(near, way))] for m, way in ((far_up, 2), (far_down, -2))
            ]
        if distance == 0:
            break
        for i, way in enumerate((1, -1)):
            at = ORDER.index(distance * way) * far
            came = [goes[i]] + (jumps[i] if distance == 2 else [])
            (goes[i],) = call(functools.partial(sum_kernel, at=at, half=i), [two], *came)
    at = ORDER.index(0) * far
    (away,) = call(functools.partial(away_kernel, at=at), [one], *goes)
    other = lax.ppermute(away, "zh", swap(far, 1))
    return pl.pallas_call(
        functools.partial(finish_kernel, at=at + 1),
        out_shape=[
            jax.ShapeDtypeStruct((blocks[2], 1, 3 * width), F32),
            jax.ShapeDtypeStruct((1, width, blocks[2]), F32),
        ],
        in_specs=[VMEM] * 5,
        out_specs=[VMEM] * 2,
        compiler_params=PARAMS,
    )(mine, theirs, *goes, other)


def solution(mesh):
    sizes = (2, mesh.shape["dp"] // 4, 2, mesh.shape["mp"] // 4, 4)
    fine = Mesh(mesh.devices.reshape(sizes), ("zh", "y", "c", "zl", "x"))
    dp, mp = ("zh", "y", "c"), ("zl", "x")
    in_specs = (P(dp + mp, None), P(dp + mp, None), P(None, mp, None), P(mp, None, None))
    out_specs = (P(dp, mp, None), P(mp, None, dp))
    return jax.shard_map(
        functools.partial(local, sizes),
        mesh=fine,
        in_specs=in_specs,
        out_specs=out_specs,
        check_vma=False,
    )
```

```python
import functools

import jax
import jax.numpy as jnp
from jax import lax
from jax.experimental import pallas as pl
from jax.experimental.pallas import tpu as pltpu
from jax.sharding import Mesh
from jax.sharding import PartitionSpec as P

HIGHEST = lax.Precision.HIGHEST
BF16 = jnp.bfloat16
F32 = jnp.float32
EPS = 1e-6
TM = (((0,), (0,)), ((), ()))
NT = (((1,), (1,)), ((), ()))
NN = (((1,), (0,)), ((), ()))
VMEM = pl.BlockSpec(memory_space=pltpu.VMEM)
SMEM = pl.BlockSpec(memory_space=pltpu.SMEM)
ORDER = (4, 3, -3, 2, -2, 1, -1, 0)
PARAMS = pltpu.CompilerParams(vmem_limit_bytes=16 * 1024 * 1024)


def normalize(values):
    centred = values - jnp.mean(values, -1, keepdims=True)
    spread = lax.rsqrt(jnp.mean(centred * centred, -1, keepdims=True) + EPS)
    return centred * spread, spread


def normalize_back(grad, normed, spread):
    inner = jnp.mean(grad * normed, -1, keepdims=True)
    return spread * (grad - jnp.mean(grad, -1, keepdims=True) - normed * inner)


def exact(a, b, dims):
    return lax.dot_general(a, b, dims, precision=HIGHEST, preferred_element_type=F32)


def normalize_rows(piece, normed_ref, at, count):
    step = 16

    def body(i, carry):
        x = piece[pl.ds(pl.multiple_of(i * step, step), step), :].astype(F32)
        centred = x - jnp.mean(x, -1, keepdims=True)
        spread = lax.rsqrt(jnp.mean(centred * centred, -1, keepdims=True) + EPS)
        rows = pl.ds(pl.multiple_of(at + i * step, step), step)
        normed_ref[rows, :] = (centred * spread).astype(BF16)
        return carry

    lax.fori_loop(0, count // step, body, 0)


def normalize_kernel(*refs):
    normed_ref, at = refs[-1], 0
    for piece in refs[:-1]:
        normalize_rows(piece, normed_ref, at, piece.shape[0])
        at += piece.shape[0]


def forward_kernel(*refs, count):
    pieces = refs[:count]
    w_ref, att_ref, q_ref, k_ref, v_ref, prob_ref, sq_ref, sk_ref = refs[count:]
    width = w_ref.shape[1] // 3
    qkv = jnp.concatenate(
        [jnp.dot(p[...], w_ref[...], preferred_element_type=F32) for p in pieces], 0
    )
    q, sq = normalize(qkv[:, :width])
    k, sk = normalize(qkv[:, width : 2 * width])
    v = qkv[:, 2 * width :]
    weights = jnp.exp(exact(q, k, NT) * width ** (-0.5))
    probs = weights / jnp.sum(weights, -1, keepdims=True)
    att_ref[...] = exact(probs, v, NN).T.astype(BF16)
    q_ref[...] = q
    k_ref[...] = k
    v_ref[...] = v
    prob_ref[...] = probs
    sq_ref[...] = jnp.broadcast_to(sq, q.shape)
    sk_ref[...] = jnp.broadcast_to(sk, k.shape)


def backward_kernel(*refs, count):
    pieces = refs[:count]
    w_ref, q_ref, k_ref, v_ref, prob_ref, sq_ref, sk_ref, out_ref = refs[count:]
    width = w_ref.shape[0]
    cot = jnp.concatenate([piece[...] for piece in pieces], 0)
    d_att = lax.dot_general(cot, w_ref[...], NT, preferred_element_type=F32)
    q, k, v, probs = q_ref[...], k_ref[...], v_ref[...], prob_ref[...]
    d_value = exact(probs, d_att, TM)
    d_probs = exact(d_att, v, NT)
    inner = jnp.sum(d_probs * probs, -1, keepdims=True)
    d_scores = probs * (d_probs - inner) * width ** (-0.5)
    d_q = normalize_back(exact(d_scores, k, NN), q, sq_ref[...])
    d_k = normalize_back(exact(d_scores, q, TM), k, sk_ref[...])
    out_ref[:width, :] = d_q.T.astype(BF16)
    out_ref[width : 2 * width, :] = d_k.T.astype(BF16)
    out_ref[2 * width :, :] = d_value.T.astype(BF16)


def terms_kernel(*refs, counts, blocks):
    place_ref, refs = refs[0], refs[1:]
    normed, pieces = refs[: counts[0]], refs[counts[0] : sum(counts)]
    d_ref, att_ref, out_ref = refs[sum(counts) :]
    far, near, width = blocks
    core, here, zh = place_ref[0], place_ref[1], place_ref[2]
    d_all, att = d_ref[...], att_ref[...]
    split = d_all.shape[0]
    for slot, distance in enumerate(ORDER):
        y = lax.rem(here + distance + near, near)
        cols = [
            pl.ds(pl.multiple_of(((z * near + y) * 2 + core) * width, width), width)
            for z in (1 - zh, zh)
        ]
        rhs = jnp.concatenate([jnp.concatenate([p[:, c] for p in normed], 0) for c in cols], 1)
        cot = jnp.concatenate([jnp.concatenate([p[:, c] for p in pieces], 0) for c in cols], 1)
        top = jnp.dot(d_all, rhs, preferred_element_type=F32)
        low = jnp.dot(att, cot, preferred_element_type=F32)
        for i in range(far):
            out_ref[slot * far + i, :split, :] = top[:, i * width : (i + 1) * width].astype(BF16)
            out_ref[slot * far + i, split:, :] = low[:, i * width : (i + 1) * width].astype(BF16)


def first_kernel(own_ref, theirs_ref, up_ref, down_ref):
    for at, out_ref in enumerate((up_ref, down_ref)):
        out_ref[...] = (own_ref[at, :, :].astype(F32) + theirs_ref[at, :, :].astype(F32)).astype(BF16)


def sum_kernel(own_ref, theirs_ref, came_ref, out_ref, *, at, half):
    for i in range(2):
        total = own_ref[at + i, :, :].astype(F32) + theirs_ref[at + i, :, :].astype(F32)
        if half is None:
            total = total + came_ref[i, :, :].astype(F32)
        elif half == i:
            total = total + came_ref[...].astype(F32)
        out_ref[i, :, :] = total.astype(BF16)


def away_kernel(own_ref, theirs_ref, up_ref, down_ref, out_ref, *, at):
    total = own_ref[at, :, :].astype(F32) + theirs_ref[at, :, :].astype(F32)
    for ref in (up_ref, down_ref):
        total = total + ref[0, :, :].astype(F32)
    out_ref[...] = total.astype(BF16)


def finish_kernel(own_ref, theirs_ref, up_ref, down_ref, other_ref, qkv_ref, out_ref, *, at):
    both = own_ref[at, :, :].astype(F32) + theirs_ref[at, :, :].astype(F32)
    for ref in (up_ref, down_ref):
        both = both + ref[1, :, :].astype(F32)
    both = both + other_ref[...].astype(F32)
    split = qkv_ref.shape[-1]
    qkv_ref[:, 0, :] = both[:split].T
    out_ref[0, :, :] = both[split:]


def swap(n, s):
    return [(i, i ^ s) for i in range(n)]


def turn(n, s):
    return [(i, (i + s) % n) for i in range(n)]


def after(value, *done):
    return lax.optimization_barrier((value, *done))[0]


def normalized(*pieces):
    rows = sum(p.shape[0] for p in pieces)
    return pl.pallas_call(
        normalize_kernel,
        out_shape=jax.ShapeDtypeStruct((rows, pieces[0].shape[1]), BF16),
        in_specs=[VMEM] * len(pieces),
        out_specs=VMEM,
        compiler_params=PARAMS,
    )(*pieces)


def gather(tokens, cotangent, n_z, n_x):
    up, down = turn(n_x, 1), turn(n_x, -1)

    def join(*rows):
        return lax.optimization_barrier(jnp.concatenate(rows, 0))

    def within(rows):
        return [lax.ppermute(rows, "zl", swap(n_z, s)) for s in (2, 3, 1)]

    t_other = lax.ppermute(tokens, "zl", swap(n_z, 4))
    t = join(tokens, t_other)
    t_near = within(t)
    c = join(cotangent, lax.ppermute(cotangent, "zl", swap(n_z, 4)))
    t = join(t, *t_near)
    t_left = lax.ppermute(t, "x", up)
    t_right = lax.ppermute(t, "x", down)
    normed = normalized(t)
    c_near = within(c)
    c = join(c, *c_near)
    t_far = lax.ppermute(t_left, "x", up)
    c_right = lax.ppermute(c, "x", down)
    c_left = lax.ppermute(after(c, t_left), "x", up)
    left = normalized(t_left)
    rest = normalized(t_right, t_far)
    c_far = lax.ppermute(c_right, "x", down)
    return [normed, left, rest], [c, c_left, c_right, c_far]


def local(sizes, tokens, cotangent, w_qkv, w_out):
    far, near, cores, n_z, n_x = sizes
    w_head = w_qkv[:, 0, :]
    w_back = w_out[0]
    model, width = w_head.shape[0], w_back.shape[0]
    normed, c_pieces = gather(tokens, cotangent, n_z, n_x)
    total = sum(p.shape[0] for p in normed)
    small = jax.ShapeDtypeStruct((total, width), F32)
    att, *saved = pl.pallas_call(
        functools.partial(forward_kernel, count=len(normed)),
        out_shape=[
            jax.ShapeDtypeStruct((width, total), BF16),
            small,
            small,
            small,
            jax.ShapeDtypeStruct((total, total), F32),
            small,
            small,
        ],
        in_specs=[VMEM] * (len(normed) + 1),
        out_specs=[VMEM] * 7,
        compiler_params=PARAMS,
    )(*normed, w_head)
    d_qkv = pl.pallas_call(
        functools.partial(backward_kernel, count=len(c_pieces)),
        out_shape=jax.ShapeDtypeStruct((3 * width, total), BF16),
        in_specs=[VMEM] * (len(c_pieces) + 7),
        out_specs=VMEM,
        compiler_params=PARAMS,
    )(*c_pieces, w_back, *saved)
    blocks = (far, near, model // (far * near * cores))
    one = jax.ShapeDtypeStruct((4 * width, blocks[2]), BF16)
    here = lax.axis_index("y").astype(jnp.int32)
    core = lax.axis_index("c").astype(jnp.int32)
    zh = lax.axis_index("zh").astype(jnp.int32)

    def terms(core):
        return pl.pallas_call(
            functools.partial(
                terms_kernel, counts=(len(normed), len(c_pieces)), blocks=blocks
            ),
            out_shape=jax.ShapeDtypeStruct((far * near, *one.shape), BF16),
            in_specs=[SMEM] + [VMEM] * (len(normed) + len(c_pieces) + 2),
            out_specs=VMEM,
            compiler_params=PARAMS,
        )(jnp.stack([core, here, zh]), *normed, *c_pieces, d_qkv, att)

    theirs = lax.ppermute(terms(1 - core), "c", swap(cores, 1))
    mine = terms(core)

    two = jax.ShapeDtypeStruct((far, *one.shape), BF16)

    def call(kernel, shapes, *came):
        return pl.pallas_call(
            kernel,
            out_shape=shapes,
            in_specs=[VMEM] * (2 + len(came)),
            out_specs=[VMEM] * len(shapes),
            compiler_params=PARAMS,
        )(mine, theirs, *came)

    goes = list(call(first_kernel, [one, one]))
    for distance in (3, 2, 1, 0):
        goes = [lax.ppermute(m, "y", turn(near, way)) for m, way in zip(goes, (1, -1))]
        if distance == 0:
            break
        for i, way in enumerate((1, -1)):
            at = ORDER.index(distance * way) * far
            half = i if distance == 3 else None
            (goes[i],) = call(functools.partial(sum_kernel, at=at, half=half), [two], goes[i])
    at = ORDER.index(0) * far
    (away,) = call(functools.partial(away_kernel, at=at), [one], *goes)
    other = lax.ppermute(away, "zh", swap(far, 1))
    return pl.pallas_call(
        functools.partial(finish_kernel, at=at + 1),
        out_shape=[
            jax.ShapeDtypeStruct((blocks[2], 1, 3 * width), F32),
            jax.ShapeDtypeStruct((1, width, blocks[2]), F32),
        ],
        in_specs=[VMEM] * 5,
        out_specs=[VMEM] * 2,
        compiler_params=PARAMS,
    )(mine, theirs, *goes, other)


def solution(mesh):
    sizes = (2, mesh.shape["dp"] // 4, 2, mesh.shape["mp"] // 4, 4)
    fine = Mesh(mesh.devices.reshape(sizes), ("zh", "y", "c", "zl", "x"))
    dp, mp = ("zh", "y", "c"), ("zl", "x")
    in_specs = (P(dp + mp, None), P(dp + mp, None), P(None, mp, None), P(mp, None, None))
    out_specs = (P(dp, mp, None), P(mp, None, dp))
    return jax.shard_map(
        functools.partial(local, sizes),
        mesh=fine,
        in_specs=in_specs,
        out_specs=out_specs,
        check_vma=False,
    )
```
